256 devices in a mesh: section: 4 (over z_hi, core), tp: 64 (over x, y, z_lo).
Axes of the slice: x: 4, y: 4, z: 8 (z_hi: 2, z_lo: 4; z = z_hi * 4 + z_lo), core: 2. Of those that a mesh axis runs over, the one named last changes fastest.
Arguments:
- travelling_inputs: bfloat16 [4, 512, 3072], P('section', 'tp'), may hold values from -6 to 6
- travelling_region: int32 [4, 512], P('section', 'tp'), may hold values 0 or 1
- arriving_tiles: bfloat16 [4, 512, 3072], P('section', 'tp'), may hold values from -6 to 6
- arriving_region: int32 [4, 512], P('section', 'tp'), may hold values 0 or 1
- prompt_embeddings: bfloat16 [2048, 3584], P(('section', 'tp')), may hold values from -6 to 6
- prompt_tally: int32 [1], replicated, may hold values from 512 to 2048
- adaptive_norm_weights: bfloat16 [4, 9216, 3584], P('section', 'tp'), may hold values from -0.09375 to 0.09375
- expansion_weights: bfloat16 [4, 12288, 3072], P('section', 'tp'), may hold values from -0.109375 to 0.109375
- contraction_weights: bfloat16 [4, 12288, 3072], P('section', 'tp'), may hold values from -0.0546875 to 0.0546875
Outputs:
- finished: bfloat16 [4, 512, 3072], P('section', 'tp')
- state: bfloat16 [4, 512, 3072], P('section', 'tp')
The draws below stay inside these ranges and needn't reach their ends.
All inputs are finite; a program needn't handle non-finite values. No bound on the sum of `travelling_region` or of `arriving_region` on one device may be relied on, other than what follows from the above.
Results may differ from the reference program's by a relative error of at most 0.01.
Values may be sent and summed in bfloat16 or wider, within the bound.
No kernel may reach another device: no remote copies, remote signals or barrier semaphores. Data moves between devices by JAX's collectives and lax.ppermute only.
A program may use at most 64 MiB of HBM per device.

```python
import jax
import jax.numpy as jnp
from jax import lax

EMBED_BREADTH = 3072
FF = 12288
E = 3584
TILE_POSITIONS = 512
DEPTH_TOTAL = 4
TEXT = 2048


def set_ends(array, stream_key, low, top_value):
    place = [jax.random.randint(jax.random.fold_in(stream_key, axis), (), 0, length) for axis, length in enumerate(array.shape)]
    longest = array.shape.index(max(array.shape))
    next_to = place[:longest] + [(place[longest] + 1) % array.shape[longest]] + place[longest + 1:]
    return array.at[tuple(place)].set(low).at[tuple(next_to)].set(top_value)


def level_of(stream_key, dims, split, smallest, top_value):
    gain = 1.0
    for dim, shards_of in split:
        draws = jax.random.uniform(jax.random.fold_in(jax.random.fold_in(stream_key, 6), dim), (shards_of,), jnp.float32, smallest / len(split), top_value / len(split))
        gain = gain * jnp.repeat(jnp.exp(draws), dims[dim] // shards_of).reshape((-1,) + (1,) * (len(dims) - 1 - dim))
    return gain


def gaussian(rng, shape, width, most, shards=(), held_as=jnp.bfloat16):
    level = level_of(rng, shape, shards, -0.22, 0.18) if shards else 1.0
    array = jax.random.normal(rng, shape, jnp.float32) * width * level
    return jnp.minimum(jnp.maximum(array, -most), most).astype(held_as)


def setup_inputs(seed: int = 0) -> dict:
    arg_keys = jax.random.split(jax.random.key(seed), 10)
    return {
        "travelling_inputs": gaussian(arg_keys[0], (DEPTH_TOTAL, TILE_POSITIONS, EMBED_BREADTH), 1.0, 6.0, ((0, 4), (1, 64))),
        "travelling_region": set_ends((jax.random.randint(arg_keys[1], (DEPTH_TOTAL, TILE_POSITIONS), 0, 2) < 1).astype(jnp.int32), jax.random.fold_in(arg_keys[1], 1), 0, 1),
        "arriving_tiles": gaussian(arg_keys[2], (DEPTH_TOTAL, TILE_POSITIONS, EMBED_BREADTH), 1.0, 6.0, ((0, 4), (1, 64))),
        "arriving_region": set_ends((jax.random.randint(arg_keys[3], (DEPTH_TOTAL, TILE_POSITIONS), 0, 2) < 1).astype(jnp.int32), jax.random.fold_in(arg_keys[3], 1), 0, 1),
        "prompt_embeddings": gaussian(arg_keys[4], (TEXT, E), 1.0, 6.0, ((0, 256),)),
        "prompt_tally": jax.random.randint(arg_keys[5], (1,), TEXT // 4, TEXT + 1).astype(jnp.int32),
        "adaptive_norm_weights": gaussian(arg_keys[6], (DEPTH_TOTAL, 3 * EMBED_BREADTH, E), E ** -0.5, 0.09375, ((0, 4), (1, 64))),
        "expansion_weights": gaussian(arg_keys[7], (DEPTH_TOTAL, FF, EMBED_BREADTH), EMBED_BREADTH ** -0.5, 0.109375, ((0, 4), (1, 64))),
        "contraction_weights": gaussian(arg_keys[8], (DEPTH_TOTAL, FF, EMBED_BREADTH), FF ** -0.5, 0.0546875, ((0, 4), (1, 64))),
    }


def layer_apply(stream, mask_row, cond, mod_weight, up_weight, down_weight):
    modes = jnp.dot(mod_weight, cond, preferred_element_type=jnp.float32)
    shift = modes[:EMBED_BREADTH]
    scale = modes[EMBED_BREADTH:2 * EMBED_BREADTH]
    gate = modes[2 * EMBED_BREADTH:]
    values = stream.astype(jnp.float32)
    center = lax.optimization_barrier(jnp.mean(values, axis=1, keepdims=True))
    spread = lax.optimization_barrier(jnp.mean((values - center) ** 2, axis=1, keepdims=True))
    normed = (values - center) * jax.lax.rsqrt(spread + 1e-06)
    inputs = (normed * (1.0 + scale) + shift).astype(jnp.bfloat16)
    hidden = jax.nn.gelu(jnp.dot(inputs, up_weight.T, preferred_element_type=jnp.float32), approximate=True).astype(jnp.bfloat16)
    result = jnp.dot(hidden, down_weight, preferred_element_type=jnp.float32)
    return (values + mask_row.astype(jnp.float32)[:, None] * gate * result).astype(jnp.bfloat16)

def reference(travelling_inputs, travelling_region, arriving_tiles, arriving_region, prompt_embeddings, prompt_tally, adaptive_norm_weights, expansion_weights, contraction_weights):
    keep = (jnp.arange(TEXT) < prompt_tally[0]).astype(jnp.bfloat16)
    pooled = jnp.dot(keep[None, :], prompt_embeddings, preferred_element_type=jnp.float32)[0]
    pooled = pooled / prompt_tally[0].astype(jnp.float32)
    normed = pooled * jax.lax.rsqrt(jnp.mean(pooled * pooled) + 1e-06)
    cond = jax.nn.silu(normed).astype(jnp.bfloat16)
    present_tile = [travelling_inputs[relay_advance] for relay_advance in range(DEPTH_TOTAL)]
    mask_list = [travelling_region[relay_advance] for relay_advance in range(DEPTH_TOTAL)]
    outputs = []
    for tick in range(DEPTH_TOTAL):
        results = [layer_apply(present_tile[relay_advance], mask_list[relay_advance], cond, adaptive_norm_weights[relay_advance], expansion_weights[relay_advance], contraction_weights[relay_advance]) for relay_advance in range(DEPTH_TOTAL)]
        outputs.append(results[DEPTH_TOTAL - 1])
        present_tile = [arriving_tiles[tick]] + results[:DEPTH_TOTAL - 1]
        mask_list = [arriving_region[tick]] + mask_list[:DEPTH_TOTAL - 1]
    return (jnp.stack(outputs), jnp.stack(present_tile))
```

```python
import functools

import jax
import jax.numpy as jnp
import numpy as np
from jax import lax
from jax.experimental import pallas as pl
from jax.experimental.pallas import tpu as pltpu
from jax.sharding import Mesh, PartitionSpec as P

f32 = jnp.float32
bf16 = jnp.bfloat16

SIZES = {"zh": 2, "core": 2, "xh": 2, "xl": 2, "yh": 2, "yl": 2, "z": 4}
SECTION = ("zh", "core")
TP = ("xh", "xl", "yh", "yl", "z")
PLANE = ("xh", "xl", "yh", "yl")
GROUP = ("xh", "z")
GROUP_SIZE = 8
SECTIONS = 4
LANES = 128


def from_neighbour(block, axis, distance):
    route = [((i + distance) % 4, i) for i in range(4)]
    return lax.ppermute(block, (axis + "h", axis + "l"), route)


def between_sections(block, edges):
    return lax.ppermute(block, SECTION, edges)


def exchange(block, axes):
    count = int(np.prod([SIZES[a] for a in axes]))
    copies = jnp.broadcast_to(block[None], (count,) + block.shape)
    return lax.all_to_all(copies, axes, 0, 0)


def ffn_kernel(pieces, half, x_ref, mod_ref, *refs):
    weights = refs[:pieces]
    out_ref, up, down, inputs, hidden, sem = refs[pieces:]
    lifts, drops = [], []
    for i, w in enumerate(weights):
        rows = pl.ds(i * half, half)
        lifts.append(pltpu.make_async_copy(w.at[pl.ds(0, half)], up.at[rows], sem.at[0, i]))
        drops.append(pltpu.make_async_copy(w.at[pl.ds(half, half)], down.at[rows], sem.at[1, i]))
    for copy in lifts:
        copy.start()
    for copy in drops:
        copy.start()
    values = x_ref[...].astype(f32)
    center = jnp.mean(values, axis=1, keepdims=True)
    moved = values - center
    spread = jnp.mean(moved * moved, axis=1, keepdims=True)
    inputs[...] = (
        moved * lax.rsqrt(spread + 1e-06) * (1.0 + mod_ref[1:2]) + mod_ref[0:1]
    ).astype(bf16)
    total = pieces * half
    step = 256
    arrived = 0
    for at in range(0, total, step):
        while arrived * half < at + step:
            lifts[arrived].wait()
            arrived += 1
        raised = lax.dot_general(
            inputs[...],
            up[at : at + step],
            (((1,), (1,)), ((), ())),
            preferred_element_type=f32,
        )
        hidden[:, at : at + step] = jax.nn.gelu(raised, approximate=True).astype(bf16)
    for copy in drops:
        copy.wait()
    for at in range(0, out_ref.shape[1], step):
        out_ref[:, at : at + step] = jnp.dot(
            hidden[...], down[:, at : at + step], preferred_element_type=f32
        ).astype(bf16)


def ffn(tokens, mod, weights):
    rows, breadth = tokens.shape
    pieces = len(weights)
    half = weights[0].shape[0] // 2
    total = pieces * half
    whole = pl.BlockSpec(memory_space=pltpu.VMEM)
    return pl.pallas_call(
        functools.partial(ffn_kernel, pieces, half),
        out_shape=jax.ShapeDtypeStruct((rows, breadth), bf16),
        in_specs=[whole, whole] + [pl.BlockSpec(memory_space=pl.ANY)] * pieces,
        out_specs=whole,
        scratch_shapes=[
            pltpu.VMEM((total, breadth), bf16),
            pltpu.VMEM((total, breadth), bf16),
            pltpu.VMEM((rows, breadth), bf16),
            pltpu.VMEM((rows, total), bf16),
            pltpu.SemaphoreType.DMA((2, pieces)),
        ],
        compiler_params=pltpu.CompilerParams(vmem_limit_bytes=40 * 1024 * 1024),
        cost_estimate=pl.CostEstimate(
            flops=4 * rows * total * breadth,
            bytes_accessed=4 * total * breadth + 4 * rows * breadth,
            transcendentals=rows * total,
        ),
    )(tokens, mod, *weights)


def spread_weights(up, down):
    middle = up.shape[0] // 2
    first = jnp.concatenate([up[:middle], down[:middle]], axis=0)
    second = jnp.concatenate([up[middle:], down[middle:]], axis=0)
    xa = from_neighbour(first, "x", 1)
    xb = from_neighbour(second, "x", -1)
    yp_first = from_neighbour(first, "y", 1)
    ym_second = from_neighbour(second, "y", -1)
    yp_second = from_neighbour(second, "y", 1)
    ym_first = from_neighbour(first, "y", -1)
    xa_yp = from_neighbour(yp_first, "x", 1)
    xb_ym = from_neighbour(ym_second, "x", -1)
    y2_first = from_neighbour(yp_first, "y", 1)
    y2_second = from_neighbour(ym_second, "y", -1)
    xa_ym = from_neighbour(ym_first, "x", 1)
    xb_yp = from_neighbour(yp_second, "x", -1)
    xa_y2 = from_neighbour(y2_first, "x", 1)
    xb_y2 = from_neighbour(y2_second, "x", -1)
    return [
        first, second, xa, xb, yp_first, ym_second, yp_second, ym_first,
        xa_yp, xb_ym, y2_first, y2_second, xa_ym, xb_yp, xa_y2, xb_y2,
    ]


def condition(prompt_embeddings, prompt_tally, adaptive_norm_weights):
    count_rows, encoded = prompt_embeddings.shape
    first_row = lax.axis_index(SECTION + TP) * count_rows
    keep = (first_row + lax.iota(jnp.int32, count_rows) < prompt_tally[0]).astype(bf16)
    partial = jnp.dot(keep[None, :], prompt_embeddings, preferred_element_type=f32)
    partial = partial.reshape(encoded // LANES, LANES)
    partial = jnp.sum(exchange(partial, PLANE), axis=0)
    pooled = jnp.sum(exchange(partial, ("zh", "core", "z")), axis=0)
    pooled = pooled / prompt_tally[0].astype(f32)
    normed = pooled * lax.rsqrt(jnp.mean(pooled * pooled) + 1e-06)
    cond = jax.nn.silu(normed).astype(bf16).reshape(encoded)
    local = jnp.dot(adaptive_norm_weights, cond, preferred_element_type=f32)
    columns = local.shape[0]
    rows = -(-columns // LANES)
    local = jnp.pad(local, (0, rows * LANES - columns)).reshape(rows, LANES)
    modes = exchange(local, TP)
    return modes.reshape(modes.shape[0], rows * LANES)[:, :columns].reshape(3, -1)


def per_device(
    travelling_inputs,
    travelling_region,
    arriving_tiles,
    arriving_region,
    prompt_embeddings,
    prompt_tally,
    adaptive_norm_weights,
    expansion_weights,
    contraction_weights,
):
    section_id = lax.axis_index(SECTION)
    is_first = section_id == 0
    tokens, breadth = travelling_inputs.shape[1:]

    def with_mask(values, region):
        column = jnp.broadcast_to(region.astype(bf16)[:, None], (tokens, LANES))
        return jnp.concatenate([values, column], axis=1)

    arriving = with_mask(arriving_tiles[0], arriving_region[0])
    waiting = with_mask(travelling_inputs[0], travelling_region[0])
    entering = [arriving] + [between_sections(arriving, [(s, 0)]) for s in range(1, SECTIONS)]
    mod = condition(prompt_embeddings, prompt_tally, adaptive_norm_weights[0])
    weights = spread_weights(expansion_weights[0], contraction_weights[0])
    finished = None
    for tick in range(SECTIONS):
        gathered = exchange(waiting[:, :breadth], GROUP)
        partial = ffn(gathered.reshape(GROUP_SIZE * tokens, breadth), mod, weights)
        parts = lax.all_to_all(partial.reshape(GROUP_SIZE, tokens, breadth), GROUP, 0, 0)
        result = jnp.sum(parts.astype(f32), axis=0)
        mask = waiting[:, breadth:]
        produced = (
            waiting[:, :breadth].astype(f32) + mask[:, :1].astype(f32) * mod[2][None] * result
        ).astype(bf16)
        produced = jnp.concatenate([produced, mask], axis=1)
        edges = [(s, s + 1) for s in range(SECTIONS - 1)]
        if tick == 0:
            moved = between_sections(produced, edges + [(SECTIONS - 1, 0)])
            finished = moved
        else:
            moved = between_sections(produced, edges)
            if tick < SECTIONS - 1:
                left = between_sections(produced[:, :breadth], [(SECTIONS - 1, tick)])
            else:
                left = produced[:, :breadth]
            finished = jnp.where(section_id == tick, left, finished[:, :breadth])
        waiting = jnp.where(is_first, entering[tick], moved)
    return finished[None], waiting[None, :, :breadth]


def solution(mesh):
    fine = Mesh(mesh.devices.reshape(tuple(SIZES.values())), tuple(SIZES))
    placed = (
        P(SECTION, TP, None),
        P(SECTION, TP),
        P(SECTION, TP, None),
        P(SECTION, TP),
        P(SECTION + TP, None),
        P(),
        P(SECTION, TP, None),
        P(SECTION, TP, None),
        P(SECTION, TP, None),
    )
    return jax.shard_map(
        per_device,
        mesh=fine,
        in_specs=placed,
        out_specs=(P(SECTION, TP, None), P(SECTION, TP, None)),
        check_vma=False,
    )
```

```python
import functools

import jax
import jax.numpy as jnp
import numpy as np
from jax import lax
from jax.experimental import pallas as pl
from jax.experimental.pallas import tpu as pltpu
from jax.sharding import Mesh, PartitionSpec as P

f32 = jnp.float32
bf16 = jnp.bfloat16

SIZES = {"zh": 2, "core": 2, "xh": 2, "xl": 2, "yh": 2, "yl": 2, "zc": 2, "zf": 2}
SECTION = ("zh", "core")
TP = ("xh", "xl", "yh", "yl", "zc", "zf")
PLANE = ("xh", "xl", "yh", "yl")
LINE = ("zc", "zf")
GROUP = ("xh",) + LINE
GROUP_SIZE = 8
SECTIONS = 4
LANES = 128


def from_neighbour(block, axis, distance):
    route = [((i + distance) % 4, i) for i in range(4)]
    return lax.ppermute(block, (axis + "h", axis + "l"), route)


def between_sections(block, edges):
    route = [
        (2 * start + half, 2 * end + (half ^ flip)) for start, end, flip in edges for half in (0, 1)
    ]
    return lax.ppermute(block, SECTION + ("zc",), route)


def after(value, *earlier):
    return lax.optimization_barrier((value,) + earlier)[0]


def exchange(block, axes):
    count = int(np.prod([SIZES[a] for a in axes]))
    copies = jnp.broadcast_to(block[None], (count,) + block.shape)
    return lax.all_to_all(copies, axes, 0, 0)


def ffn_kernel(pieces, half, x_ref, mod_ref, *refs):
    weights = refs[:pieces]
    out_ref, up, down, inputs, hidden, acc, sem = refs[pieces:]
    lifts, drops = [], []
    for i, w in enumerate(weights):
        rows = pl.ds(i * half, half)
        lifts.append(pltpu.make_async_copy(w.at[pl.ds(0, half)], up.at[rows], sem.at[0, i]))
        drops.append(pltpu.make_async_copy(w.at[pl.ds(half, half)], down.at[rows], sem.at[1, i]))
    for copy in lifts:
        copy.start()
    for copy in drops:
        copy.start()
    values = x_ref[...].astype(f32)
    center = jnp.mean(values, axis=1, keepdims=True)
    moved = values - center
    spread = jnp.mean(moved * moved, axis=1, keepdims=True)
    inputs[...] = (
        moved * lax.rsqrt(spread + 1e-06) * (1.0 + mod_ref[1:2]) + mod_ref[0:1]
    ).astype(bf16)
    total = pieces * half
    step = 256
    arrived = 0
    for at in range(0, total, step):
        while arrived * half < at + step:
            lifts[arrived].wait()
            arrived += 1
        raised = lax.dot_general(
            inputs[...],
            up[at : at + step],
            (((1,), (1,)), ((), ())),
            preferred_element_type=f32,
        )
        hidden[:, at : at + step] = jax.nn.gelu(raised, approximate=True).astype(bf16)
    arrived = 0
    for at in range(0, total, step):
        while arrived * half < at + step:
            drops[arrived].wait()
            arrived += 1
        for column in range(0, out_ref.shape[1], step):
            columns = slice(column, column + step)
            term = jnp.dot(
                hidden[:, at : at + step], down[at : at + step, columns], preferred_element_type=f32
            )
            if at:
                term = acc[:, columns] + term
            if at + step < total:
                acc[:, columns] = term
            else:
                out_ref[:, columns] = term.astype(bf16)


def ffn(tokens, mod, weights):
    rows, breadth = tokens.shape
    pieces = len(weights)
    half = weights[0].shape[0] // 2
    total = pieces * half
    whole = pl.BlockSpec(memory_space=pltpu.VMEM)
    return pl.pallas_call(
        functools.partial(ffn_kernel, pieces, half),
        out_shape=jax.ShapeDtypeStruct((rows, breadth), bf16),
        in_specs=[whole, whole] + [pl.BlockSpec(memory_space=pl.ANY)] * pieces,
        out_specs=whole,
        scratch_shapes=[
            pltpu.VMEM((total, breadth), bf16),
            pltpu.VMEM((total, breadth), bf16),
            pltpu.VMEM((rows, breadth), bf16),
            pltpu.VMEM((rows, total), bf16),
            pltpu.VMEM((rows, breadth), f32),
            pltpu.SemaphoreType.DMA((2, pieces)),
        ],
        compiler_params=pltpu.CompilerParams(vmem_limit_bytes=40 * 1024 * 1024),
        cost_estimate=pl.CostEstimate(
            flops=4 * rows * total * breadth,
            bytes_accessed=4 * total * breadth + 4 * rows * breadth,
            transcendentals=rows * total,
        ),
    )(tokens, mod, *weights)


def close_kernel(parts_ref, waiting_ref, gate_ref, out_ref):
    breadth = parts_ref.shape[2]
    result = parts_ref[0].astype(f32)
    for i in range(1, parts_ref.shape[0]):
        result += parts_ref[i].astype(f32)
    mask = waiting_ref[:, breadth:]
    kept = mask[:, :1].astype(f32)
    values = waiting_ref[:, :breadth].astype(f32)
    out_ref[:, :breadth] = (values + kept * gate_ref[...] * result).astype(bf16)
    out_ref[:, breadth:] = mask


def close(parts, waiting, gate):
    whole = pl.BlockSpec(memory_space=pltpu.VMEM)
    return pl.pallas_call(
        close_kernel,
        out_shape=jax.ShapeDtypeStruct(waiting.shape, waiting.dtype),
        in_specs=[whole] * 3,
        out_specs=whole,
        cost_estimate=pl.CostEstimate(
            flops=parts.size, bytes_accessed=2 * parts.size, transcendentals=0
        ),
    )(parts, waiting, gate)


def set_out(up, down, prompt_embeddings, prompt_tally, adaptive_norm_weights, waiting):
    middle = up.shape[0] // 2
    first = jnp.concatenate([up[:middle], down[:middle]], axis=0)
    second = jnp.concatenate([up[middle:], down[middle:]], axis=0)
    count_rows, encoded = prompt_embeddings.shape
    first_row = lax.axis_index(SECTION + TP) * count_rows
    keep = (first_row + lax.iota(jnp.int32, count_rows) < prompt_tally[0]).astype(bf16)
    partial = jnp.dot(keep[None, :], prompt_embeddings, preferred_element_type=f32)
    partial = partial.reshape(encoded // LANES, LANES)
    partial = jnp.sum(exchange(partial, PLANE), axis=0)

    first, second = after((first, second), partial)
    yp_first = from_neighbour(first, "y", 1)
    ym_second = from_neighbour(second, "y", -1)
    xa = from_neighbour(first, "x", 1)
    xb = from_neighbour(second, "x", -1)
    yp_second = from_neighbour(second, "y", 1)
    ym_first = from_neighbour(first, "y", -1)

    pooled = jnp.sum(exchange(partial, SECTION + LINE), axis=0)
    yp_first, ym_second = after((yp_first, ym_second), pooled)
    xa_yp = from_neighbour(yp_first, "x", 1)
    xb_ym = from_neighbour(ym_second, "x", -1)

    pooled = pooled / prompt_tally[0].astype(f32)
    normed = pooled * lax.rsqrt(jnp.mean(pooled * pooled) + 1e-06)
    cond = jax.nn.silu(normed).astype(bf16).reshape(encoded)
    local = jnp.dot(adaptive_norm_weights, cond, preferred_element_type=f32)
    columns = local.shape[0]
    rows = -(-columns // LANES)
    local = jnp.pad(local, (0, rows * LANES - columns)).reshape(rows, LANES)
    line = exchange(local, LINE)

    yp_first, ym_second, yp_second, ym_first = after(
        (yp_first, ym_second, yp_second, ym_first), line
    )
    y2_first = from_neighbour(yp_first, "y", 1)
    y2_second = from_neighbour(ym_second, "y", -1)
    xa_ym = from_neighbour(ym_first, "x", 1)
    xb_yp = from_neighbour(yp_second, "x", -1)
    xa_y2 = from_neighbour(y2_first, "x", 1)
    xb_y2 = from_neighbour(y2_second, "x", -1)

    modes = exchange(line, PLANE)
    modes = modes.reshape(-1, rows * LANES)[:, :columns].reshape(3, -1)

    waiting = after(waiting, line)
    mine = exchange(waiting, LINE)
    theirs = lax.ppermute(mine, "xh", [(0, 1), (1, 0)])
    upper = lax.axis_index("xh") == 1
    gathered = jnp.stack([jnp.where(upper, theirs, mine), jnp.where(upper, mine, theirs)])
    pieces = [
        first, second, xa, xb, yp_first, ym_second, yp_second, ym_first,
        xa_yp, xb_ym, y2_first, y2_second, xa_ym, xb_yp, xa_y2, xb_y2,
    ]
    return modes, gathered, pieces


def per_device(
    travelling_inputs,
    travelling_region,
    arriving_tiles,
    arriving_region,
    prompt_embeddings,
    prompt_tally,
    adaptive_norm_weights,
    expansion_weights,
    contraction_weights,
):
    section_id = lax.axis_index(SECTION)
    is_first = section_id == 0
    tokens, breadth = travelling_inputs.shape[1:]

    def with_mask(values, region):
        column = jnp.broadcast_to(region.astype(bf16)[:, None], (tokens, LANES))
        return jnp.concatenate([values, column], axis=1)

    arriving = with_mask(arriving_tiles[0], arriving_region[0])
    waiting = with_mask(travelling_inputs[0], travelling_region[0])
    last = SECTIONS - 1
    entering = [arriving]
    for section in range(1, SECTIONS):
        entering.append(between_sections(arriving, [(section, 0, 0)]))
    mod, gathered, weights = set_out(
        expansion_weights[0],
        contraction_weights[0],
        prompt_embeddings,
        prompt_tally,
        adaptive_norm_weights[0],
        travelling_inputs[0],
    )
    finished = []
    for tick in range(SECTIONS):
        if tick:
            gathered = exchange(waiting[:, :breadth], GROUP)
        partial = ffn(gathered.reshape(GROUP_SIZE * tokens, breadth), mod, weights)
        parts = lax.all_to_all(partial.reshape(GROUP_SIZE, tokens, breadth), GROUP, 0, 0)
        produced = close(parts, waiting, mod[2:])
        if tick < last:
            moved = between_sections(produced, [(0, 1, 0), (1, 2, 1), (2, 3, 0)])
            flip = int(tick >= 2)
            finished.append(between_sections(produced[:, :breadth], [(last, tick, flip)]))
        else:
            moved = between_sections(produced, [(0, 1, 0), (1, 2, 0), (2, 3, 1)])
            finished.append(between_sections(produced[:, :breadth], [(last, last, 1)]))
        waiting = jnp.where(is_first, entering[tick], moved)
    done = finished[last]
    for tick in range(last):
        done = jnp.where(section_id == tick, finished[tick], done)
    return done[None], waiting[None, :, :breadth]


def solution(mesh):
    fine = Mesh(mesh.devices.reshape(tuple(SIZES.values())), tuple(SIZES))
    placed = (
        P(SECTION, TP, None),
        P(SECTION, TP),
        P(SECTION, TP, None),
        P(SECTION, TP),
        P(SECTION + TP, None),
        P(),
        P(SECTION, TP, None),
        P(SECTION, TP, None),
        P(SECTION, TP, None),
    )
    return jax.shard_map(
        per_device,
        mesh=fine,
        in_specs=placed,
        out_specs=(P(SECTION, TP, None), P(SECTION, TP, None)),
        check_vma=False,
    )
```

```python
import functools

import jax
import jax.numpy as jnp
import numpy as np
from jax import lax
from jax.experimental import pallas as pl
from jax.experimental.pallas import tpu as pltpu
from jax.sharding import Mesh, PartitionSpec as P

f32 = jnp.float32
bf16 = jnp.bfloat16

SIZES = {"zh": 2, "core": 2, "xh": 2, "xl": 2, "yh": 2, "yl": 2, "zc": 2, "zf": 2}
SECTION = ("zh", "core")
TP = ("xh", "xl", "yh", "yl", "zc", "zf")
PLANE = ("xh", "xl", "yh", "yl")
LINE = ("zc", "zf")
GROUP = ("xh",) + LINE
GROUP_SIZE = 8
SECTIONS = 4
LANES = 128
STEP = 256
IN_FLIGHT = 6


def from_neighbour(block, axis, distance):
    route = [((i + distance) % 4, i) for i in range(4)]
    return lax.ppermute(block, (axis + "h", axis + "l"), route)


def between_sections(block, edges):
    route = [
        (2 * start + half, 2 * end + (half ^ flip)) for start, end, flip in edges for half in (0, 1)
    ]
    return lax.ppermute(block, SECTION + ("zc",), route)


def after(value, *earlier):
    return lax.optimization_barrier((value,) + earlier)[0]


def exchange(block, axes):
    count = int(np.prod([SIZES[a] for a in axes]))
    copies = jnp.broadcast_to(block[None], (count,) + block.shape)
    return lax.all_to_all(copies, axes, 0, 0)


def ffn_kernel(lifts, drops, x_ref, mod_ref, *refs):
    held = len({i for i, _, _ in lifts + drops})
    weights = refs[:held]
    out_ref, up, down, inputs, hidden, acc, sem = refs[held:]
    copies = []
    for place, parts in ((up, lifts), (down, drops)):
        at = 0
        for i, first, rows in parts:
            copies.append(
                pltpu.make_async_copy(
                    weights[i].at[pl.ds(first, rows)],
                    place.at[pl.ds(at, rows)],
                    sem.at[len(copies)],
                )
            )
            at += rows
    total = at
    for copy in copies[:IN_FLIGHT]:
        copy.start()
    values = x_ref[...].astype(f32)
    center = jnp.mean(values, axis=1, keepdims=True)
    moved = values - center
    spread = jnp.mean(moved * moved, axis=1, keepdims=True)
    inputs[...] = (
        moved * lax.rsqrt(spread + 1e-06) * (1.0 + mod_ref[1:2]) + mod_ref[0:1]
    ).astype(bf16)
    ready = 0

    def wait_for(rows, skip, parts):
        nonlocal ready
        while sum(part[2] for part in parts[: ready - skip]) < rows:
            copies[ready].wait()
            if ready + IN_FLIGHT < len(copies):
                copies[ready + IN_FLIGHT].start()
            ready += 1

    for at in range(0, total, STEP):
        wait_for(at + STEP, 0, lifts)
        raised = lax.dot_general(
            inputs[...],
            up[at : at + STEP],
            (((1,), (1,)), ((), ())),
            preferred_element_type=f32,
        )
        hidden[:, at : at + STEP] = jax.nn.gelu(raised, approximate=True).astype(bf16)
    for at in range(0, total, STEP):
        wait_for(at + STEP, len(lifts), drops)
        for column in range(0, out_ref.shape[1], STEP):
            columns = slice(column, column + STEP)
            term = jnp.dot(
                hidden[:, at : at + STEP], down[at : at + STEP, columns], preferred_element_type=f32
            )
            if at:
                term = acc[:, columns] + term
            if at + STEP < total:
                acc[:, columns] = term
            else:
                out_ref[:, columns] = term.astype(bf16)


def ffn(tokens, mod, weights, lifts, drops):
    rows, breadth = tokens.shape
    total = sum(part[2] for part in lifts)
    whole = pl.BlockSpec(memory_space=pltpu.VMEM)
    return pl.pallas_call(
        functools.partial(ffn_kernel, lifts, drops),
        out_shape=jax.ShapeDtypeStruct((rows, breadth), bf16),
        in_specs=[whole, whole] + [pl.BlockSpec(memory_space=pltpu.HBM)] * len(weights),
        out_specs=whole,
        scratch_shapes=[
            pltpu.VMEM((total, breadth), bf16),
            pltpu.VMEM((total, breadth), bf16),
            pltpu.VMEM((rows, breadth), bf16),
            pltpu.VMEM((rows, total), bf16),
            pltpu.VMEM((rows, breadth), f32),
            pltpu.SemaphoreType.DMA((len(lifts) + len(drops),)),
        ],
        compiler_params=pltpu.CompilerParams(vmem_limit_bytes=40 * 1024 * 1024),
        cost_estimate=pl.CostEstimate(
            flops=4 * rows * total * breadth,
            bytes_accessed=4 * total * breadth + 4 * rows * breadth,
            transcendentals=rows * total,
        ),
    )(tokens, mod, *weights)


def close_kernel(parts_ref, waiting_ref, gate_ref, out_ref):
    breadth = parts_ref.shape[2]
    result = parts_ref[0].astype(f32)
    for i in range(1, parts_ref.shape[0]):
        result += parts_ref[i].astype(f32)
    mask = waiting_ref[:, breadth:]
    kept = mask[:, :1].astype(f32)
    values = waiting_ref[:, :breadth].astype(f32)
    out_ref[:, :breadth] = (values + kept * gate_ref[...] * result).astype(bf16)
    out_ref[:, breadth:] = mask


def close(parts, waiting, gate):
    whole = pl.BlockSpec(memory_space=pltpu.VMEM)
    return pl.pallas_call(
        close_kernel,
        out_shape=jax.ShapeDtypeStruct(waiting.shape, waiting.dtype),
        in_specs=[whole] * 3,
        out_specs=whole,
        cost_estimate=pl.CostEstimate(
            flops=parts.size, bytes_accessed=2 * parts.size, transcendentals=0
        ),
    )(parts, waiting, gate)


def ring_gather(block, axis):
    blocks = [block] + [from_neighbour(block, axis, d) for d in (1, 2, 3)]
    me = lax.axis_index((axis + "h", axis + "l"))

    def held_by(place):
        found = blocks[place]
        for at in (1, 2, 3):
            found = jnp.where(me == at, blocks[(place - at) % 4], found)
        return found

    return jnp.stack([held_by(place) for place in range(4)])


def set_out(up, down, prompt_embeddings, prompt_tally, adaptive_norm_weights, waiting):
    middle = up.shape[0] // 2
    first = jnp.concatenate([up[:middle], down[:middle]], axis=0)
    second = jnp.concatenate([up[middle:], down[middle:]], axis=0)
    count_rows, encoded = prompt_embeddings.shape
    first_row = lax.axis_index(SECTION + TP) * count_rows
    keep = (first_row + lax.iota(jnp.int32, count_rows) < prompt_tally[0]).astype(bf16)
    partial = jnp.dot(keep[None, :], prompt_embeddings, preferred_element_type=f32)
    partial = partial.reshape(encoded // LANES, LANES)
    partial = jnp.sum(exchange(partial, PLANE), axis=0)

    first, second = after((first, second), partial)
    yp_first = from_neighbour(first, "y", 1)
    ym_second = from_neighbour(second, "y", -1)
    xa = from_neighbour(first, "x", 1)
    xb = from_neighbour(second, "x", -1)

    pooled = jnp.sum(exchange(partial, SECTION + LINE), axis=0)
    mine = exchange(after(waiting, pooled), LINE)

    first, second, yp_first, ym_second, xa, xb, _, pooled = lax.optimization_barrier(
        (first, second, yp_first, ym_second, xa, xb, mine, pooled)
    )
    yp_second = from_neighbour(second, "y", 1)
    ym_first = from_neighbour(first, "y", -1)
    xa_yp = from_neighbour(yp_first, "x", 1)
    xb_ym = from_neighbour(ym_second, "x", -1)

    pooled = pooled / prompt_tally[0].astype(f32)
    normed = pooled * lax.rsqrt(jnp.mean(pooled * pooled) + 1e-06)
    cond = jax.nn.silu(normed).astype(bf16).reshape(encoded)
    local = jnp.dot(adaptive_norm_weights, cond, preferred_element_type=f32)
    columns = local.shape[0]
    rows = -(-columns // LANES)
    local = jnp.pad(local, (0, rows * LANES - columns)).reshape(rows, LANES)
    line = exchange(local, LINE)
    modes = ring_gather(ring_gather(line, "y"), "x")
    modes = modes.reshape(-1, rows * LANES)[:, :columns].reshape(3, -1)
    theirs = lax.ppermute(mine, "xh", [(0, 1), (1, 0)])
    upper = lax.axis_index("xh") == 1
    gathered = jnp.stack([jnp.where(upper, theirs, mine), jnp.where(upper, mine, theirs)])

    yp_first, ym_second, yp_second, ym_first, xa_yp, xb_ym = after(
        (yp_first, ym_second, yp_second, ym_first, xa_yp, xb_ym), line
    )
    y2_first = from_neighbour(yp_first, "y", 1)
    y2_second = from_neighbour(ym_second, "y", -1)
    xa_ym = from_neighbour(ym_first, "x", 1)
    xb_yp = from_neighbour(yp_second, "x", -1)

    y2_first, y2_second, xa_ym, xb_yp = lax.optimization_barrier(
        (y2_first, y2_second, xa_ym, xb_yp)
    )
    xa_y2_up = from_neighbour(y2_first[:middle], "x", 1)
    xb_y2_up = from_neighbour(y2_second[:middle], "x", -1)
    xa_y2_down = from_neighbour(xa_yp[middle:], "y", 1)
    xb_y2_down = from_neighbour(xb_ym[middle:], "y", -1)

    whole = [
        first, second, xa, xb, yp_first, ym_second, yp_second, ym_first,
        xa_yp, xb_ym, y2_first, y2_second, xa_ym, xb_yp,
    ]
    count = len(whole)
    lifts = [(i, 0, middle) for i in range(count)]
    drops = [(i, middle, middle) for i in range(count)]
    lifts += [(count, 0, middle), (count + 1, 0, middle)]
    drops += [(count + 2, 0, middle), (count + 3, 0, middle)]
    weights = whole + [xa_y2_up, xb_y2_up, xa_y2_down, xb_y2_down]
    return modes, gathered, functools.partial(ffn, weights=weights, lifts=lifts, drops=drops)


def per_device(
    travelling_inputs,
    travelling_region,
    arriving_tiles,
    arriving_region,
    prompt_embeddings,
    prompt_tally,
    adaptive_norm_weights,
    expansion_weights,
    contraction_weights,
):
    section_id = lax.axis_index(SECTION)
    is_first = section_id == 0
    tokens, breadth = travelling_inputs.shape[1:]

    def with_mask(values, region):
        column = jnp.broadcast_to(region.astype(bf16)[:, None], (tokens, LANES))
        return jnp.concatenate([values, column], axis=1)

    arriving = with_mask(arriving_tiles[0], arriving_region[0])
    waiting = with_mask(travelling_inputs[0], travelling_region[0])
    last = SECTIONS - 1
    entering = [arriving]
    for section in range(1, SECTIONS):
        entering.append(between_sections(arriving, [(section, 0, 0)]))
    mod, gathered, layer = set_out(
        expansion_weights[0],
        contraction_weights[0],
        prompt_embeddings,
        prompt_tally,
        adaptive_norm_weights[0],
        travelling_inputs[0],
    )
    gathered, waiting, gate, *entering = lax.optimization_barrier(
        (gathered, waiting, mod[2:], *entering)
    )
    finished = []
    for tick in range(SECTIONS):
        if tick:
            gathered = exchange(waiting[:, :breadth], GROUP)
        partial = layer(gathered.reshape(GROUP_SIZE * tokens, breadth), mod)
        parts = lax.all_to_all(partial.reshape(GROUP_SIZE, tokens, breadth), GROUP, 0, 0)
        produced = close(parts, waiting, gate)
        if tick < last:
            moved = between_sections(produced, [(0, 1, 0), (1, 2, 1), (2, 3, 0)])
            flip = int(tick >= 2)
            finished.append(between_sections(produced, [(last, tick, flip)]))
        else:
            moved = between_sections(produced, [(0, 1, 0), (1, 2, 0), (2, 3, 1)])
            finished.append(between_sections(produced, [(last, last, 1)]))
        waiting = jnp.where(is_first, entering[tick], moved)
    done = finished[last]
    for tick in range(last):
        done = jnp.where(section_id == tick, finished[tick], done)
    return done[None, :, :breadth], waiting[None, :, :breadth]


def solution(mesh):
    fine = Mesh(mesh.devices.reshape(tuple(SIZES.values())), tuple(SIZES))
    placed = (
        P(SECTION, TP, None),
        P(SECTION, TP),
        P(SECTION, TP, None),
        P(SECTION, TP),
        P(SECTION + TP, None),
        P(),
        P(SECTION, TP, None),
        P(SECTION, TP, None),
        P(SECTION, TP, None),
    )
    return jax.shard_map(
        per_device,
        mesh=fine,
        in_specs=placed,
        out_specs=(P(SECTION, TP, None), P(SECTION, TP, None)),
        check_vma=False,
    )
```

```python
import functools

import jax
import jax.numpy as jnp
import numpy as np
from jax import lax
from jax.experimental import pallas as pl
from jax.experimental.pallas import tpu as pltpu
from jax.sharding import Mesh, PartitionSpec as P

f32 = jnp.float32
bf16 = jnp.bfloat16

SIZES = {"zh": 2, "core": 2, "xh": 2, "xl": 2, "yh": 2, "yl": 2, "zc": 2, "zf": 2}
SECTION = ("zh", "core")
TP = ("xh", "xl", "yh", "yl", "zc", "zf")
PLANE = ("xh", "xl", "yh", "yl")
LINE = ("zc", "zf")
GROUP = ("xh",) + LINE
GROUP_SIZE = 8
SECTIONS = 4
LANES = 128
STEP = 256
SPAN = 768
IN_FLIGHT = 10


def from_neighbour(block, axis, distance):
    route = [((i + distance) % 4, i) for i in range(4)]
    return lax.ppermute(block, (axis + "h", axis + "l"), route)


def between_sections(block, edges):
    route = [
        (2 * start + half, 2 * end + (half ^ flip)) for start, end, flip in edges for half in (0, 1)
    ]
    return lax.ppermute(block, SECTION + ("zc",), route)


def after(value, *earlier):
    return lax.optimization_barrier((value,) + earlier)[0]


def exchange(block, axes):
    count = int(np.prod([SIZES[a] for a in axes]))
    copies = jnp.broadcast_to(block[None], (count,) + block.shape)
    return lax.all_to_all(copies, axes, 0, 0)


def ffn_kernel(lifts, drops, x_ref, mod_ref, *refs):
    held = len({i for i, _, _ in lifts + drops})
    weights = refs[:held]
    out_ref, up, down, inputs, hidden, acc, sem = refs[held:]
    copies = []
    for place, parts in ((up, lifts), (down, drops)):
        at = 0
        for i, first, rows in parts:
            copies.append(
                pltpu.make_async_copy(
                    weights[i].at[pl.ds(first, rows)],
                    place.at[pl.ds(at, rows)],
                    sem.at[len(copies)],
                )
            )
            at += rows
    total = at
    for copy in copies[:IN_FLIGHT]:
        copy.start()
    values = x_ref[...].astype(f32)
    center = jnp.mean(values, axis=1, keepdims=True)
    moved = values - center
    spread = jnp.mean(moved * moved, axis=1, keepdims=True)
    inputs[...] = (
        moved * lax.rsqrt(spread + 1e-06) * (1.0 + mod_ref[1:2]) + mod_ref[0:1]
    ).astype(bf16)
    ready = 0

    def wait_for(rows, skip, parts):
        nonlocal ready
        while sum(part[2] for part in parts[: ready - skip]) < rows:
            copies[ready].wait()
            if ready + IN_FLIGHT < len(copies):
                copies[ready + IN_FLIGHT].start()
            ready += 1

    for span in range(0, total, SPAN):
        wait_for(span + SPAN, 0, lifts)
        for at in range(span, span + SPAN, STEP):
            raised = lax.dot_general(
                inputs[...],
                up[at : at + STEP],
                (((1,), (1,)), ((), ())),
                preferred_element_type=f32,
            )
            hidden[:, at : at + STEP] = jax.nn.gelu(raised, approximate=True).astype(bf16)
    for at in range(0, total, SPAN):
        wait_for(at + SPAN, len(lifts), drops)
        for column in range(0, out_ref.shape[1], STEP):
            columns = slice(column, column + STEP)
            term = jnp.dot(
                hidden[:, at : at + SPAN], down[at : at + SPAN, columns], preferred_element_type=f32
            )
            if at:
                term = acc[:, columns] + term
            if at + SPAN < total:
                acc[:, columns] = term
            else:
                out_ref[:, columns] = term.astype(bf16)


def ffn(tokens, mod, weights, lifts, drops):
    rows, breadth = tokens.shape
    total = sum(part[2] for part in lifts)
    whole = pl.BlockSpec(memory_space=pltpu.VMEM)
    return pl.pallas_call(
        functools.partial(ffn_kernel, lifts, drops),
        out_shape=jax.ShapeDtypeStruct((rows, breadth), bf16),
        in_specs=[whole, whole] + [pl.BlockSpec(memory_space=pltpu.HBM)] * len(weights),
        out_specs=whole,
        scratch_shapes=[
            pltpu.VMEM((total, breadth), bf16),
            pltpu.VMEM((total, breadth), bf16),
            pltpu.VMEM((rows, breadth), bf16),
            pltpu.VMEM((rows, total), bf16),
            pltpu.VMEM((rows, breadth), f32),
            pltpu.SemaphoreType.DMA((len(lifts) + len(drops),)),
        ],
        compiler_params=pltpu.CompilerParams(vmem_limit_bytes=40 * 1024 * 1024),
        cost_estimate=pl.CostEstimate(
            flops=4 * rows * total * breadth,
            bytes_accessed=4 * total * breadth + 4 * rows * breadth,
            transcendentals=rows * total,
        ),
    )(tokens, mod, *weights)


def close_kernel(parts_ref, waiting_ref, gate_ref, out_ref):
    breadth = parts_ref.shape[2]
    result = parts_ref[0].astype(f32)
    for i in range(1, parts_ref.shape[0]):
        result += parts_ref[i].astype(f32)
    mask = waiting_ref[:, breadth:]
    kept = mask[:, :1].astype(f32)
    values = waiting_ref[:, :breadth].astype(f32)
    out_ref[:, :breadth] = (values + kept * gate_ref[...] * result).astype(bf16)
    out_ref[:, breadth:] = mask


def close(parts, waiting, gate):
    whole = pl.BlockSpec(memory_space=pltpu.VMEM)
    return pl.pallas_call(
        close_kernel,
        out_shape=jax.ShapeDtypeStruct(waiting.shape, waiting.dtype),
        in_specs=[whole] * 3,
        out_specs=whole,
        cost_estimate=pl.CostEstimate(
            flops=parts.size, bytes_accessed=2 * parts.size, transcendentals=0
        ),
    )(parts, waiting, gate)


def set_out(up, down, prompt_embeddings, prompt_tally, adaptive_norm_weights, waiting, arriving):
    together = lax.optimization_barrier
    middle = up.shape[0] // 2
    first = jnp.concatenate([up[:middle], down[:middle]], axis=0)
    second = jnp.concatenate([up[middle:], down[middle:]], axis=0)
    count_rows, encoded = prompt_embeddings.shape
    first_row = lax.axis_index(SECTION + TP) * count_rows
    keep = (first_row + lax.iota(jnp.int32, count_rows) < prompt_tally[0]).astype(bf16)
    partial = jnp.dot(keep[None, :], prompt_embeddings, preferred_element_type=f32)
    partial = partial.reshape(encoded // LANES, LANES)

    first, second, partial = together((first, second, partial))
    yp_first = from_neighbour(first, "y", 1)
    ym_second = from_neighbour(second, "y", -1)
    xa = from_neighbour(first, "x", 1)
    xb = from_neighbour(second, "x", -1)
    partial = jnp.sum(exchange(partial, SECTION + LINE), axis=0)
    entering = exchange(after(arriving, partial), SECTION)

    first, second, yp_first, ym_second, xa, xb, partial, entering = together(
        (first, second, yp_first, ym_second, xa, xb, partial, entering)
    )
    pooled = jnp.sum(exchange(partial, PLANE), axis=0)

    first, second, yp_first, ym_second, pooled = together(
        (first, second, yp_first, ym_second, pooled)
    )
    yp_second = from_neighbour(second, "y", 1)
    ym_first = from_neighbour(first, "y", -1)
    xa_yp = from_neighbour(yp_first, "x", 1)
    xb_ym = from_neighbour(ym_second, "x", -1)
    pooled = pooled / prompt_tally[0].astype(f32)
    normed = pooled * lax.rsqrt(jnp.mean(pooled * pooled) + 1e-06)
    cond = jax.nn.silu(normed).astype(bf16).reshape(encoded)
    local = jnp.dot(adaptive_norm_weights, cond, preferred_element_type=f32)
    columns = local.shape[0]
    rows = -(-columns // LANES)
    local = jnp.pad(local, (0, rows * LANES - columns)).reshape(rows, LANES)
    line = exchange(local, LINE)
    mine = exchange(after(waiting, line), LINE)
    halves = [block[part] for block in (yp_first, ym_second) for part in (slice(middle), slice(middle, None))]

    line, mine, halves, yp_second, ym_first, xa_yp, xb_ym = together(
        (line, mine, halves, yp_second, ym_first, xa_yp, xb_ym)
    )
    theirs = lax.ppermute(mine, "xh", [(0, 1), (1, 0)])
    modes = exchange(line, PLANE)
    modes, theirs, halves, yp_second, ym_first = together(
        (modes, theirs, halves, yp_second, ym_first)
    )
    y2 = [from_neighbour(half, "y", 1 if i < 2 else -1) for i, half in enumerate(halves)]
    xa_ym = from_neighbour(ym_first, "x", 1)
    xb_yp = from_neighbour(yp_second, "x", -1)
    modes = modes.reshape(-1, rows * LANES)[:, :columns].reshape(3, -1)
    upper = lax.axis_index("xh") == 1
    gathered = jnp.stack([jnp.where(upper, theirs, mine), jnp.where(upper, mine, theirs)])
    xa_yp_down = xa_yp[middle:]
    xb_ym_down = xb_ym[middle:]

    y2, xa_ym, xb_yp, modes, gathered, xa_yp_down, xb_ym_down = together(
        (y2, xa_ym, xb_yp, modes, gathered, xa_yp_down, xb_ym_down)
    )
    xa_y2_up = from_neighbour(y2[0], "x", 1)
    xb_y2_up = from_neighbour(y2[2], "x", -1)
    xa_y2_down = from_neighbour(xa_yp_down, "y", 1)
    xb_y2_down = from_neighbour(xb_ym_down, "y", -1)

    whole = [
        first, second, xa, xb, yp_first, ym_second, yp_second, ym_first, xa_yp, xb_ym, xa_ym, xb_yp
    ]
    count = len(whole)
    lifts = [(i, 0, middle) for i in range(count)]
    drops = [(i, middle, middle) for i in range(count)]
    lifts += [(count + i, 0, middle) for i in (0, 2, 4, 5)]
    drops += [(count + i, 0, middle) for i in (1, 3, 6, 7)]
    weights = whole + y2 + [xa_y2_up, xb_y2_up, xa_y2_down, xb_y2_down]
    layer = functools.partial(ffn, weights=weights, lifts=lifts, drops=drops)
    return modes, gathered, entering, layer


def per_device(
    travelling_inputs,
    travelling_region,
    arriving_tiles,
    arriving_region,
    prompt_embeddings,
    prompt_tally,
    adaptive_norm_weights,
    expansion_weights,
    contraction_weights,
):
    section_id = lax.axis_index(SECTION)
    is_first = section_id == 0
    tokens, breadth = travelling_inputs.shape[1:]

    def with_mask(values, region):
        column = jnp.broadcast_to(region.astype(bf16)[:, None], (tokens, LANES))
        return jnp.concatenate([values, column], axis=1)

    arriving = with_mask(arriving_tiles[0], arriving_region[0])
    waiting = with_mask(travelling_inputs[0], travelling_region[0])
    last = SECTIONS - 1
    mod, gathered, entering, layer = set_out(
        expansion_weights[0],
        contraction_weights[0],
        prompt_embeddings,
        prompt_tally,
        adaptive_norm_weights[0],
        travelling_inputs[0],
        arriving,
    )
    gathered, waiting, gate = lax.optimization_barrier((gathered, waiting, mod[2:]))
    finished = []
    for tick in range(SECTIONS):
        if tick:
            gathered = exchange(waiting[:, :breadth], GROUP)
        partial = layer(gathered.reshape(GROUP_SIZE * tokens, breadth), mod)
        parts = lax.all_to_all(partial.reshape(GROUP_SIZE, tokens, breadth), GROUP, 0, 0)
        produced = close(parts, waiting, gate)
        if tick < last:
            moved = between_sections(produced, [(0, 1, 0), (1, 2, 1), (2, 3, 0)])
            flip = int(tick >= 2)
            finished.append(between_sections(produced, [(last, tick, flip)]))
        else:
            moved = between_sections(produced, [(0, 1, 0), (1, 2, 0), (2, 3, 1)])
            finished.append(between_sections(produced, [(last, last, 1)]))
        waiting = jnp.where(is_first, entering[tick], moved)
    done = finished[last]
    for tick in range(last):
        done = jnp.where(section_id == tick, finished[tick], done)
    return done[None, :, :breadth], waiting[None, :, :breadth]


def solution(mesh):
    fine = Mesh(mesh.devices.reshape(tuple(SIZES.values())), tuple(SIZES))
    placed = (
        P(SECTION, TP, None),
        P(SECTION, TP),
        P(SECTION, TP, None),
        P(SECTION, TP),
        P(SECTION + TP, None),
        P(),
        P(SECTION, TP, None),
        P(SECTION, TP, None),
        P(SECTION, TP, None),
    )
    return jax.shard_map(
        per_device,
        mesh=fine,
        in_specs=placed,
        out_specs=(P(SECTION, TP, None), P(SECTION, TP, None)),
        check_vma=False,
    )
```

```python
import functools

import jax
import jax.numpy as jnp
import numpy as np
from jax import lax
from jax.experimental import pallas as pl
from jax.experimental.pallas import tpu as pltpu
from jax.sharding import Mesh, PartitionSpec as P

f32 = jnp.float32
bf16 = jnp.bfloat16

SIZES = {"zh": 2, "core": 2, "xh": 2, "xl": 2, "yh": 2, "yl": 2, "zc": 2, "zf": 2}
SECTION = ("zh", "core")
TP = ("xh", "xl", "yh", "yl", "zc", "zf")
PLANE = ("xh", "xl", "yh", "yl")
LINE = ("zc", "zf")
GROUP = ("xh",) + LINE
GROUP_SIZE = 8
SECTIONS = 4
LANES = 128
STEP = 256
IN_FLIGHT = 10


def from_neighbour(block, axis, distance):
    route = [((i + distance) % 4, i) for i in range(4)]
    return lax.ppermute(block, (axis + "h", axis + "l"), route)


def between_sections(block, edges):
    route = [
        (2 * start + half, 2 * end + (half ^ flip)) for start, end, flip in edges for half in (0, 1)
    ]
    return lax.ppermute(block, SECTION + ("zc",), route)


def after(value, *earlier):
    return lax.optimization_barrier((value,) + earlier)[0]


def exchange(block, axes):
    count = int(np.prod([SIZES[a] for a in axes]))
    copies = jnp.broadcast_to(block[None], (count,) + block.shape)
    return lax.all_to_all(copies, axes, 0, 0)


def modulate(x_ref, mod_ref, inputs):
    values = x_ref[...].astype(f32)
    center = jnp.mean(values, axis=1, keepdims=True)
    moved = values - center
    spread = jnp.mean(moved * moved, axis=1, keepdims=True)
    inputs[...] = (
        moved * lax.rsqrt(spread + 1e-06) * (1.0 + mod_ref[1:2]) + mod_ref[0:1]
    ).astype(bf16)


def raise_rows(inputs, up, hidden, start, stop):
    for at in range(start, stop, STEP):
        raised = lax.dot_general(
            inputs[...],
            up[at : at + STEP],
            (((1,), (1,)), ((), ())),
            preferred_element_type=f32,
        )
        hidden[:, at : at + STEP] = jax.nn.gelu(raised, approximate=True).astype(bf16)


def lower_rows(hidden, down, out_ref):
    for at in range(0, out_ref.shape[1], STEP):
        out_ref[:, at : at + STEP] = jnp.dot(
            hidden[...], down[:, at : at + STEP], preferred_element_type=f32
        ).astype(bf16)


def first_kernel(lifts, drops, x_ref, mod_ref, *refs):
    held = len({i for i, _, _ in lifts + drops})
    weights = refs[:held]
    out_ref, up, down, inputs, hidden, sem = refs[held:]
    copies = []
    for place, parts in ((up, lifts), (down, drops)):
        at = 0
        for i, first, rows in parts:
            copies.append(
                pltpu.make_async_copy(
                    weights[i].at[pl.ds(first, rows)],
                    place.at[pl.ds(at, rows)],
                    sem.at[len(copies)],
                )
            )
            at += rows
    total = at
    for copy in copies[:IN_FLIGHT]:
        copy.start()
    modulate(x_ref, mod_ref, inputs)
    ready = 0
    half = len(lifts) // 2
    for stop in (half, len(lifts), len(copies)):
        while ready < stop:
            copies[ready].wait()
            if ready + IN_FLIGHT < len(copies):
                copies[ready + IN_FLIGHT].start()
            ready += 1
        if stop == half:
            raise_rows(inputs, up, hidden, 0, total // 2)
        elif stop == len(lifts):
            raise_rows(inputs, up, hidden, total // 2, total)
    lower_rows(hidden, down, out_ref)


def later_kernel(x_ref, mod_ref, up, down, out_ref, inputs, hidden):
    modulate(x_ref, mod_ref, inputs)
    raise_rows(inputs, up, hidden, 0, up.shape[0])
    lower_rows(hidden, down, out_ref)


def layer_call(kernel, tokens, mod, weights, pieces, total, semaphores):
    rows, breadth = tokens.shape
    whole = pl.BlockSpec(memory_space=pltpu.VMEM)
    outs = [jax.ShapeDtypeStruct((rows, breadth), bf16)]
    if pieces:
        outs += [jax.ShapeDtypeStruct((total, breadth), bf16)] * 2
    space = pl.BlockSpec(memory_space=pltpu.HBM) if pieces else whole
    return pl.pallas_call(
        kernel,
        out_shape=outs,
        in_specs=[whole, whole] + [space] * len(weights),
        out_specs=[whole] * len(outs),
        scratch_shapes=[
            pltpu.VMEM((rows, breadth), bf16),
            pltpu.VMEM((rows, total), bf16),
        ]
        + semaphores,
        compiler_params=pltpu.CompilerParams(vmem_limit_bytes=24 * 1024 * 1024),
        cost_estimate=pl.CostEstimate(
            flops=4 * rows * total * breadth,
            bytes_accessed=4 * total * breadth + 4 * rows * breadth,
            transcendentals=rows * total,
        ),
    )(tokens, mod, *weights)


def first_layer(tokens, mod, weights, lifts, drops):
    total = sum(part[2] for part in lifts)
    kernel = functools.partial(first_kernel, lifts, drops)
    semaphores = [pltpu.SemaphoreType.DMA((len(lifts) + len(drops),))]
    return layer_call(kernel, tokens, mod, weights, True, total, semaphores)


def later_layer(tokens, mod, up, down):
    return layer_call(later_kernel, tokens, mod, (up, down), False, up.shape[0], [])[0]


def close_kernel(parts_ref, waiting_ref, gate_ref, out_ref):
    breadth = parts_ref.shape[2]
    result = parts_ref[0].astype(f32)
    for i in range(1, parts_ref.shape[0]):
        result += parts_ref[i].astype(f32)
    mask = waiting_ref[:, breadth:]
    kept = mask[:, :1].astype(f32)
    values = waiting_ref[:, :breadth].astype(f32)
    out_ref[:, :breadth] = (values + kept * gate_ref[...] * result).astype(bf16)
    out_ref[:, breadth:] = mask


def close(parts, waiting, gate):
    whole = pl.BlockSpec(memory_space=pltpu.VMEM)
    return pl.pallas_call(
        close_kernel,
        out_shape=jax.ShapeDtypeStruct(waiting.shape, waiting.dtype),
        in_specs=[whole] * 3,
        out_specs=whole,
        cost_estimate=pl.CostEstimate(
            flops=parts.size, bytes_accessed=2 * parts.size, transcendentals=0
        ),
    )(parts, waiting, gate)


def set_out(up, down, prompt_embeddings, prompt_tally, adaptive_norm_weights, waiting, arriving):
    together = lax.optimization_barrier
    middle = up.shape[0] // 2
    first = jnp.concatenate([up[:middle], down[:middle]], axis=0)
    second = jnp.concatenate([up[middle:], down[middle:]], axis=0)
    count_rows, encoded = prompt_embeddings.shape
    first_row = lax.axis_index(SECTION + TP) * count_rows
    keep = (first_row + lax.iota(jnp.int32, count_rows) < prompt_tally[0]).astype(bf16)
    partial = jnp.dot(keep[None, :], prompt_embeddings, preferred_element_type=f32)
    partial = partial.reshape(encoded // LANES, LANES)

    first, second, partial = together((first, second, partial))
    yp_first = from_neighbour(first, "y", 1)
    ym_second = from_neighbour(second, "y", -1)
    xa = from_neighbour(first, "x", 1)
    xb = from_neighbour(second, "x", -1)
    partial = jnp.sum(exchange(partial, SECTION + LINE), axis=0)
    entering = exchange(after(arriving, partial), SECTION)

    first, second, yp_first, ym_second, xa, xb, partial, entering = together(
        (first, second, yp_first, ym_second, xa, xb, partial, entering)
    )
    pooled = jnp.sum(exchange(partial, PLANE), axis=0)

    first, second, yp_first, ym_second, pooled = together(
        (first, second, yp_first, ym_second, pooled)
    )
    yp_second = from_neighbour(second, "y", 1)
    ym_first = from_neighbour(first, "y", -1)
    xa_yp = from_neighbour(yp_first, "x", 1)
    xb_ym = from_neighbour(ym_second, "x", -1)
    pooled = pooled / prompt_tally[0].astype(f32)
    normed = pooled * lax.rsqrt(jnp.mean(pooled * pooled) + 1e-06)
    cond = jax.nn.silu(normed).astype(bf16).reshape(encoded)
    local = jnp.dot(adaptive_norm_weights, cond, preferred_element_type=f32)
    columns = local.shape[0]
    rows = -(-columns // LANES)
    local = jnp.pad(local, (0, rows * LANES - columns)).reshape(rows, LANES)
    line = exchange(local, LINE)
    mine = exchange(after(waiting, line), LINE)
    halves = [block[part] for block in (yp_first, ym_second) for part in (slice(middle), slice(middle, None))]

    line, mine, halves, yp_second, ym_first, xa_yp, xb_ym = together(
        (line, mine, halves, yp_second, ym_first, xa_yp, xb_ym)
    )
    theirs = lax.ppermute(mine, "xh", [(0, 1), (1, 0)])
    modes = exchange(line, PLANE)
    y2 = [from_neighbour(half, "y", 1 if i < 2 else -1) for i, half in enumerate(halves)]
    xa_ym = from_neighbour(ym_first, "x", 1)
    xb_yp = from_neighbour(yp_second, "x", -1)
    modes = modes.reshape(-1, rows * LANES)[:, :columns].reshape(3, -1)
    upper = lax.axis_index("xh") == 1
    gathered = jnp.stack([jnp.where(upper, theirs, mine), jnp.where(upper, mine, theirs)])
    xa_yp_down = xa_yp[middle:]
    xb_ym_down = xb_ym[middle:]

    y2, xa_ym, xb_yp, xa_yp_down, xb_ym_down = together(
        (y2, xa_ym, xb_yp, xa_yp_down, xb_ym_down)
    )
    xa_y2_up = from_neighbour(y2[0], "x", 1)
    xb_y2_up = from_neighbour(y2[2], "x", -1)
    xa_y2_down = from_neighbour(xa_yp_down, "y", 1)
    xb_y2_down = from_neighbour(xb_ym_down, "y", -1)

    whole = [
        first, second, xa, xb, yp_first, ym_second, yp_second, ym_first, xa_yp, xb_ym, xa_ym, xb_yp
    ]
    count = len(whole)
    lifts = [(i, 0, middle) for i in range(count)]
    drops = [(i, middle, middle) for i in range(count)]
    lifts += [(count + i, 0, middle) for i in (0, 2, 4, 5)]
    drops += [(count + i, 0, middle) for i in (1, 3, 6, 7)]
    weights = whole + y2 + [xa_y2_up, xb_y2_up, xa_y2_down, xb_y2_down]
    layer = functools.partial(first_layer, weights=weights, lifts=lifts, drops=drops)
    return modes, gathered, entering, layer


def per_device(
    travelling_inputs,
    travelling_region,
    arriving_tiles,
    arriving_region,
    prompt_embeddings,
    prompt_tally,
    adaptive_norm_weights,
    expansion_weights,
    contraction_weights,
):
    section_id = lax.axis_index(SECTION)
    is_first = section_id == 0
    tokens, breadth = travelling_inputs.shape[1:]

    def with_mask(values, region):
        column = jnp.broadcast_to(region.astype(bf16)[:, None], (tokens, LANES))
        return jnp.concatenate([values, column], axis=1)

    arriving = with_mask(arriving_tiles[0], arriving_region[0])
    waiting = with_mask(travelling_inputs[0], travelling_region[0])
    last = SECTIONS - 1
    mod, gathered, entering, layer = set_out(
        expansion_weights[0],
        contraction_weights[0],
        prompt_embeddings,
        prompt_tally,
        adaptive_norm_weights[0],
        travelling_inputs[0],
        arriving,
    )
    gathered, waiting, gate = lax.optimization_barrier((gathered, waiting, mod[2:]))
    finished = []
    for tick in range(SECTIONS):
        if tick:
            gathered = exchange(waiting[:, :breadth], GROUP)
            gathered, finished[-1] = lax.optimization_barrier((gathered, finished[-1]))
        gathered = gathered.reshape(GROUP_SIZE * tokens, breadth)
        if tick:
            partial = later_layer(gathered, mod, up, down)
        else:
            partial, up, down = layer(gathered, mod)
        parts = lax.all_to_all(partial.reshape(GROUP_SIZE, tokens, breadth), GROUP, 0, 0)
        produced = close(parts, waiting, gate)
        if tick < last:
            moved = between_sections(produced, [(0, 1, 0), (1, 2, 1), (2, 3, 0)])
            flip = int(tick >= 2)
            finished.append(between_sections(produced, [(last, tick, flip)]))
        else:
            moved = between_sections(produced, [(0, 1, 0), (1, 2, 0), (2, 3, 1)])
            finished.append(between_sections(produced, [(last, last, 1)]))
        waiting = jnp.where(is_first, entering[tick], moved)
    done = finished[last]
    for tick in range(last):
        done = jnp.where(section_id == tick, finished[tick], done)
    return done[None, :, :breadth], waiting[None, :, :breadth]


def solution(mesh):
    fine = Mesh(mesh.devices.reshape(tuple(SIZES.values())), tuple(SIZES))
    placed = (
        P(SECTION, TP, None),
        P(SECTION, TP),
        P(SECTION, TP, None),
        P(SECTION, TP),
        P(SECTION + TP, None),
        P(),
        P(SECTION, TP, None),
        P(SECTION, TP, None),
        P(SECTION, TP, None),
    )
    return jax.shard_map(
        per_device,
        mesh=fine,
        in_specs=placed,
        out_specs=(P(SECTION, TP, None), P(SECTION, TP, None)),
        check_vma=False,
    )
```

```python
import functools

import jax
import jax.numpy as jnp
import numpy as np
from jax import lax
from jax.experimental import pallas as pl
from jax.experimental.pallas import tpu as pltpu
from jax.sharding import Mesh, PartitionSpec as P

f32 = jnp.float32
bf16 = jnp.bfloat16

SIZES = {"zh": 2, "core": 2, "xh": 2, "xl": 2, "yh": 2, "yl": 2, "zc": 2, "zf": 2}
SECTION = ("zh", "core")
TP = ("xh", "xl", "yh", "yl", "zc", "zf")
PLANE = ("xh", "xl", "yh", "yl")
LINE = ("zc", "zf")
GROUP = ("xh",) + LINE
GROUP_SIZE = 8
SECTIONS = 4
LANES = 128
STEP = 256


def from_neighbour(block, axis, distance):
    route = [((i + distance) % 4, i) for i in range(4)]
    return lax.ppermute(block, (axis + "h", axis + "l"), route)


def between_sections(block, edges):
    route = [
        (2 * start + half, 2 * end + (half ^ flip)) for start, end, flip in edges for half in (0, 1)
    ]
    return lax.ppermute(block, SECTION + ("zc",), route)


def after(value, *earlier):
    return lax.optimization_barrier((value,) + earlier)[0]


def exchange(block, axes):
    count = int(np.prod([SIZES[a] for a in axes]))
    copies = jnp.broadcast_to(block[None], (count,) + block.shape)
    return lax.all_to_all(copies, axes, 0, 0)


def modulate(x_ref, mod_ref, inputs):
    values = x_ref[...].astype(f32)
    center = jnp.mean(values, axis=1, keepdims=True)
    moved = values - center
    spread = jnp.mean(moved * moved, axis=1, keepdims=True)
    inputs[...] = (
        moved * lax.rsqrt(spread + 1e-06) * (1.0 + mod_ref[1:2]) + mod_ref[0:1]
    ).astype(bf16)


def layer_kernel(x_ref, mod_ref, up, down, up_end, down_end, out_ref, inputs, hidden):
    modulate(x_ref, mod_ref, inputs)
    main = up.shape[0]
    total = main + up_end.shape[0]
    for at in range(0, total, STEP):
        rows = up[at : at + STEP] if at < main else up_end[at - main : at - main + STEP]
        raised = lax.dot_general(
            inputs[...], rows, (((1,), (1,)), ((), ())), preferred_element_type=f32
        )
        hidden[:, at : at + STEP] = jax.nn.gelu(raised, approximate=True).astype(bf16)
    for at in range(0, out_ref.shape[1], STEP):
        columns = slice(at, at + STEP)
        result = jnp.dot(hidden[:, :main], down[:, columns], preferred_element_type=f32)
        result += jnp.dot(hidden[:, main:], down_end[:, columns], preferred_element_type=f32)
        out_ref[:, columns] = result.astype(bf16)


def layer(tokens, mod, up, down, up_end, down_end):
    rows, breadth = tokens.shape
    total = up.shape[0] + up_end.shape[0]
    whole = pl.BlockSpec(memory_space=pltpu.VMEM)
    return pl.pallas_call(
        layer_kernel,
        out_shape=jax.ShapeDtypeStruct((rows, breadth), bf16),
        in_specs=[whole] * 6,
        out_specs=whole,
        scratch_shapes=[
            pltpu.VMEM((rows, breadth), bf16),
            pltpu.VMEM((rows, total), bf16),
        ],
        compiler_params=pltpu.CompilerParams(vmem_limit_bytes=24 * 1024 * 1024),
        cost_estimate=pl.CostEstimate(
            flops=4 * rows * total * breadth,
            bytes_accessed=4 * total * breadth + 4 * rows * breadth,
            transcendentals=rows * total,
        ),
    )(tokens, mod, up, down, up_end, down_end)


def place_kernel(plan, *refs):
    sem = refs[-1]
    outs = refs[-3:-1]
    copies = []
    for piece, first, rows, which, at in plan:
        copies.append(
            pltpu.make_async_copy(
                refs[piece].at[pl.ds(first, rows)],
                outs[which].at[pl.ds(at, rows)],
                sem.at[len(copies)],
            )
        )
    for copy in copies:
        copy.start()
    for copy in copies:
        copy.wait()


def place(plan, pieces, total):
    breadth = pieces[0].shape[1]
    whole = pl.BlockSpec(memory_space=pltpu.VMEM)
    return pl.pallas_call(
        functools.partial(place_kernel, plan),
        out_shape=[jax.ShapeDtypeStruct((total, breadth), bf16)] * 2,
        in_specs=[pl.BlockSpec(memory_space=pl.ANY)] * len(pieces),
        out_specs=[whole] * 2,
        scratch_shapes=[pltpu.SemaphoreType.DMA((len(plan),))],
        compiler_params=pltpu.CompilerParams(vmem_limit_bytes=20 * 1024 * 1024),
        cost_estimate=pl.CostEstimate(
            flops=0, bytes_accessed=8 * total * breadth, transcendentals=0
        ),
    )(*pieces)


def close_kernel(parts_ref, waiting_ref, gate_ref, out_ref):
    breadth = parts_ref.shape[2]
    result = parts_ref[0].astype(f32)
    for i in range(1, parts_ref.shape[0]):
        result += parts_ref[i].astype(f32)
    mask = waiting_ref[:, breadth:]
    kept = mask[:, :1].astype(f32)
    values = waiting_ref[:, :breadth].astype(f32)
    out_ref[:, :breadth] = (values + kept * gate_ref[...] * result).astype(bf16)
    out_ref[:, breadth:] = mask


def close(parts, waiting, gate):
    whole = pl.BlockSpec(memory_space=pltpu.VMEM)
    return pl.pallas_call(
        close_kernel,
        out_shape=jax.ShapeDtypeStruct(waiting.shape, waiting.dtype),
        in_specs=[whole] * 3,
        out_specs=whole,
        cost_estimate=pl.CostEstimate(
            flops=parts.size, bytes_accessed=2 * parts.size, transcendentals=0
        ),
    )(parts, waiting, gate)


def set_out(up, down, prompt_embeddings, prompt_tally, adaptive_norm_weights, waiting, arriving):
    together = lax.optimization_barrier
    middle = up.shape[0] // 2
    first = jnp.concatenate([up[:middle], down[:middle]], axis=0)
    second = jnp.concatenate([up[middle:], down[middle:]], axis=0)
    count_rows, encoded = prompt_embeddings.shape
    first_row = lax.axis_index(SECTION + TP) * count_rows
    keep = (first_row + lax.iota(jnp.int32, count_rows) < prompt_tally[0]).astype(bf16)
    partial = jnp.dot(keep[None, :], prompt_embeddings, preferred_element_type=f32)
    partial = partial.reshape(encoded // LANES, LANES)

    first, second, partial = together((first, second, partial))
    yp_first = from_neighbour(first, "y", 1)
    ym_second = from_neighbour(second, "y", -1)
    xa = from_neighbour(first, "x", 1)
    xb = from_neighbour(second, "x", -1)
    partial = jnp.sum(exchange(partial, SECTION + LINE), axis=0)

    first, second, yp_first, ym_second, xa, xb, partial = together(
        (first, second, yp_first, ym_second, xa, xb, partial)
    )
    pooled = jnp.sum(exchange(partial, PLANE), axis=0)

    first, second, yp_first, ym_second, pooled = together(
        (first, second, yp_first, ym_second, pooled)
    )
    yp_second = from_neighbour(second, "y", 1)
    ym_first = from_neighbour(first, "y", -1)
    xa_yp = from_neighbour(yp_first, "x", 1)
    xb_ym = from_neighbour(ym_second, "x", -1)
    pooled = pooled / prompt_tally[0].astype(f32)
    normed = pooled * lax.rsqrt(jnp.mean(pooled * pooled) + 1e-06)
    cond = jax.nn.silu(normed).astype(bf16).reshape(encoded)
    local = jnp.dot(adaptive_norm_weights, cond, preferred_element_type=f32)
    columns = local.shape[0]
    rows = -(-columns // LANES)
    local = jnp.pad(local, (0, rows * LANES - columns)).reshape(rows, LANES)
    line = exchange(local, LINE)
    mine = exchange(after(waiting, line), LINE)
    halves = [block[part] for block in (yp_first, ym_second) for part in (slice(middle), slice(middle, None))]

    line, mine, halves, yp_second, ym_first, xa_yp, xb_ym = together(
        (line, mine, halves, yp_second, ym_first, xa_yp, xb_ym)
    )
    y2 = [from_neighbour(half, "y", 1 if i < 2 else -1) for i, half in enumerate(halves)]
    xa_ym = from_neighbour(ym_first, "x", 1)
    xb_yp = from_neighbour(yp_second, "x", -1)
    theirs = lax.ppermute(mine, "xh", [(0, 1), (1, 0)])
    entering = exchange(after(arriving, mine), SECTION)
    xa_yp_down = xa_yp[middle:]
    xb_ym_down = xb_ym[middle:]

    y2, xa_ym, xb_yp, xa_yp_down, xb_ym_down, entering, line = together(
        (y2, xa_ym, xb_yp, xa_yp_down, xb_ym_down, entering, line)
    )
    xa_y2_up = from_neighbour(y2[0], "x", 1)
    xb_y2_up = from_neighbour(y2[2], "x", -1)
    xa_y2_down = from_neighbour(xa_yp_down, "y", 1)
    xb_y2_down = from_neighbour(xb_ym_down, "y", -1)

    whole = [
        first, second, xa, xb, yp_first, ym_second, yp_second, ym_first, xa_yp, xb_ym, xa_ym, xb_yp
    ]
    count = len(whole)
    total = (count + 4) * middle
    main = (total - 1) // STEP * STEP
    cut = main - (count + 1) * middle
    plan = [
        (i, which * middle, middle, which, i * middle) for i in range(count) for which in (0, 1)
    ]
    plan += [(count + which, 0, middle, which, count * middle) for which in (0, 1)]
    plan += [(count + 2 + which, 0, cut, which, main - cut) for which in (0, 1)]
    up_rows, down_rows = place(plan, whole + y2, main)
    modes = exchange(after(line, up_rows), PLANE)
    modes = modes.reshape(-1, rows * LANES)[:, :columns].reshape(3, -1)
    upper = lax.axis_index("xh") == 1
    gathered = jnp.stack([jnp.where(upper, theirs, mine), jnp.where(upper, mine, theirs)])
    plan = [(which, cut, middle - cut, which, 0) for which in (0, 1)]
    plan += [
        (2 + 2 * which + i, 0, middle, which, (1 + i) * middle - cut)
        for which in (0, 1)
        for i in (0, 1)
    ]
    ends = [y2[2], y2[3], xa_y2_up, xb_y2_up, xa_y2_down, xb_y2_down]
    up_end, down_end = place(plan, ends, total - main)
    return modes, gathered, entering, (up_rows, down_rows, up_end, down_end)


def per_device(
    travelling_inputs,
    travelling_region,
    arriving_tiles,
    arriving_region,
    prompt_embeddings,
    prompt_tally,
    adaptive_norm_weights,
    expansion_weights,
    contraction_weights,
):
    section_id = lax.axis_index(SECTION)
    is_first = section_id == 0
    tokens, breadth = travelling_inputs.shape[1:]

    def with_mask(values, region):
        column = jnp.broadcast_to(region.astype(bf16)[:, None], (tokens, LANES))
        return jnp.concatenate([values, column], axis=1)

    arriving = with_mask(arriving_tiles[0], arriving_region[0])
    waiting = with_mask(travelling_inputs[0], travelling_region[0])
    last = SECTIONS - 1
    mod, gathered, entering, weights = set_out(
        expansion_weights[0],
        contraction_weights[0],
        prompt_embeddings,
        prompt_tally,
        adaptive_norm_weights[0],
        travelling_inputs[0],
        arriving,
    )
    gathered, waiting, gate = lax.optimization_barrier((gathered, waiting, mod[2:]))
    moves = []
    for tick in range(SECTIONS):
        if tick:
            gathered = exchange(waiting[:, :breadth], GROUP)
        partial = layer(gathered.reshape(GROUP_SIZE * tokens, breadth), mod, *weights)
        parts = lax.all_to_all(partial.reshape(GROUP_SIZE, tokens, breadth), GROUP, 0, 0)
        if tick == last:
            third = between_sections(after(produced, parts), [(last, 2, 1)])
        produced = close(parts, waiting, gate)
        if tick < last:
            edges = [(0, 1, 0), (1, 2, 1), (2, 3, 0)]
            if tick < 2:
                edges.append((last, 0, 0))
        else:
            edges = [(0, 1, 0), (1, 2, 0), (2, 3, 1)]
        moves.append(between_sections(produced, edges))
        waiting = jnp.where(is_first, entering[tick], moves[tick])
    sent = jnp.where(is_first, moves[1], produced)
    second = between_sections(sent, [(0, 1, 0), (last, last, 1)])
    done = jnp.where(is_first, moves[0], jnp.where(section_id == 2, third, second))
    return done[None, :, :breadth], waiting[None, :, :breadth]


def solution(mesh):
    fine = Mesh(mesh.devices.reshape(tuple(SIZES.values())), tuple(SIZES))
    placed = (
        P(SECTION, TP, None),
        P(SECTION, TP),
        P(SECTION, TP, None),
        P(SECTION, TP),
        P(SECTION + TP, None),
        P(),
        P(SECTION, TP, None),
        P(SECTION, TP, None),
        P(SECTION, TP, None),
    )
    return jax.shard_map(
        per_device,
        mesh=fine,
        in_specs=placed,
        out_specs=(P(SECTION, TP, None), P(SECTION, TP, None)),
        check_vma=False,
    )
```

```python
import functools

import jax
import jax.numpy as jnp
import numpy as np
from jax import lax
from jax.experimental import pallas as pl
from jax.experimental.pallas import tpu as pltpu
from jax.sharding import Mesh, PartitionSpec as P

f32 = jnp.float32
bf16 = jnp.bfloat16

SIZES = {"zh": 2, "core": 2, "xh": 2, "xl": 2, "yh": 2, "yl": 2, "zc": 2, "zf": 2}
SECTION = ("zh", "core")
TP = ("xh", "xl", "yh", "yl", "zc", "zf")
PLANE = ("xh", "xl", "yh", "yl")
LINE = ("zc", "zf")
GROUP = ("xh",) + LINE
GROUP_SIZE = 8
SECTIONS = 4
LANES = 128
STEP = 256


def from_neighbour(block, axis, distance):
    route = [((i + distance) % 4, i) for i in range(4)]
    return lax.ppermute(block, (axis + "h", axis + "l"), route)


def between_sections(block, edges):
    route = [
        (2 * start + half, 2 * end + (half ^ flip)) for start, end, flip in edges for half in (0, 1)
    ]
    return lax.ppermute(block, SECTION + ("zc",), route)


def after(value, *earlier):
    return lax.optimization_barrier((value,) + earlier)[0]


def exchange(block, axes):
    count = int(np.prod([SIZES[a] for a in axes]))
    copies = jnp.broadcast_to(block[None], (count,) + block.shape)
    return lax.all_to_all(copies, axes, 0, 0)


def modulate(x_ref, mod_ref, inputs):
    values = x_ref[...].astype(f32)
    center = jnp.mean(values, axis=1, keepdims=True)
    moved = values - center
    spread = jnp.mean(moved * moved, axis=1, keepdims=True)
    inputs[...] = (
        moved * lax.rsqrt(spread + 1e-06) * (1.0 + mod_ref[1:2]) + mod_ref[0:1]
    ).astype(bf16)


def layer_kernel(x_ref, mod_ref, up, down, up_end, down_end, out_ref, inputs, hidden):
    modulate(x_ref, mod_ref, inputs)
    main = up.shape[0]
    total = main + up_end.shape[0]
    for at in range(0, total, STEP):
        rows = up[at : at + STEP] if at < main else up_end[at - main : at - main + STEP]
        raised = lax.dot_general(
            inputs[...], rows, (((1,), (1,)), ((), ())), preferred_element_type=f32
        )
        hidden[:, at : at + STEP] = jax.nn.gelu(raised, approximate=True).astype(bf16)
    for at in range(0, out_ref.shape[1], STEP):
        columns = slice(at, at + STEP)
        result = jnp.dot(hidden[:, :main], down[:, columns], preferred_element_type=f32)
        result += jnp.dot(hidden[:, main:], down_end[:, columns], preferred_element_type=f32)
        out_ref[:, columns] = result.astype(bf16)


def layer(tokens, mod, up, down, up_end, down_end):
    rows, breadth = tokens.shape
    total = up.shape[0] + up_end.shape[0]
    whole = pl.BlockSpec(memory_space=pltpu.VMEM)
    return pl.pallas_call(
        layer_kernel,
        out_shape=jax.ShapeDtypeStruct((rows, breadth), bf16),
        in_specs=[whole] * 6,
        out_specs=whole,
        scratch_shapes=[
            pltpu.VMEM((rows, breadth), bf16),
            pltpu.VMEM((rows, total), bf16),
        ],
        compiler_params=pltpu.CompilerParams(vmem_limit_bytes=24 * 1024 * 1024),
        cost_estimate=pl.CostEstimate(
            flops=4 * rows * total * breadth,
            bytes_accessed=4 * total * breadth + 4 * rows * breadth,
            transcendentals=rows * total,
        ),
    )(tokens, mod, up, down, up_end, down_end)


def place_kernel(plan, *refs):
    sem = refs[-1]
    outs = refs[-3:-1]
    copies = []
    for piece, first, rows, which, at in plan:
        copies.append(
            pltpu.make_async_copy(
                refs[piece].at[pl.ds(first, rows)],
                outs[which].at[pl.ds(at, rows)],
                sem.at[len(copies)],
            )
        )
    for copy in copies:
        copy.start()
    for copy in copies:
        copy.wait()


def place(plan, pieces, total):
    breadth = pieces[0].shape[1]
    whole = pl.BlockSpec(memory_space=pltpu.VMEM)
    return pl.pallas_call(
        functools.partial(place_kernel, plan),
        out_shape=[jax.ShapeDtypeStruct((total, breadth), bf16)] * 2,
        in_specs=[pl.BlockSpec(memory_space=pl.ANY)] * len(pieces),
        out_specs=[whole] * 2,
        scratch_shapes=[pltpu.SemaphoreType.DMA((len(plan),))],
        compiler_params=pltpu.CompilerParams(vmem_limit_bytes=20 * 1024 * 1024),
        cost_estimate=pl.CostEstimate(
            flops=0, bytes_accessed=8 * total * breadth, transcendentals=0
        ),
    )(*pieces)


def close_kernel(parts_ref, waiting_ref, gate_ref, out_ref):
    breadth = parts_ref.shape[2]
    result = parts_ref[0].astype(f32)
    for i in range(1, parts_ref.shape[0]):
        result += parts_ref[i].astype(f32)
    mask = waiting_ref[:, breadth:]
    kept = mask[:, :1].astype(f32)
    values = waiting_ref[:, :breadth].astype(f32)
    out_ref[:, :breadth] = (values + kept * gate_ref[...] * result).astype(bf16)
    out_ref[:, breadth:] = mask


def close(parts, waiting, gate):
    whole = pl.BlockSpec(memory_space=pltpu.VMEM)
    return pl.pallas_call(
        close_kernel,
        out_shape=jax.ShapeDtypeStruct(waiting.shape, waiting.dtype),
        in_specs=[whole] * 3,
        out_specs=whole,
        compiler_params=pltpu.CompilerParams(vmem_limit_bytes=4 * 1024 * 1024),
        cost_estimate=pl.CostEstimate(
            flops=parts.size, bytes_accessed=2 * parts.size, transcendentals=0
        ),
    )(parts, waiting, gate)


def set_out(up, down, prompt_embeddings, prompt_tally, adaptive_norm_weights, waiting, arriving):
    together = lax.optimization_barrier
    middle = up.shape[0] // 2
    first = jnp.concatenate([up[:middle], down[:middle]], axis=0)
    second = jnp.concatenate([up[middle:], down[middle:]], axis=0)
    count_rows, encoded = prompt_embeddings.shape
    first_row = lax.axis_index(SECTION + TP) * count_rows
    keep = (first_row + lax.iota(jnp.int32, count_rows) < prompt_tally[0]).astype(bf16)
    partial = jnp.dot(keep[None, :], prompt_embeddings, preferred_element_type=f32)
    partial = partial.reshape(encoded // LANES, LANES)

    first, second, partial = together((first, second, partial))
    yp_first = from_neighbour(first, "y", 1)
    ym_second = from_neighbour(second, "y", -1)
    xa = from_neighbour(first, "x", 1)
    xb = from_neighbour(second, "x", -1)
    partial = jnp.sum(exchange(partial, SECTION + LINE), axis=0)
    entering = exchange(after(arriving, partial), SECTION)
    entering = [entering[section] for section in range(SECTIONS)]

    first, second, yp_first, ym_second, xa, xb, partial, entering = together(
        (first, second, yp_first, ym_second, xa, xb, partial, entering)
    )
    pooled = jnp.sum(exchange(partial, PLANE), axis=0)

    first, second, yp_first, ym_second, pooled = together(
        (first, second, yp_first, ym_second, pooled)
    )
    yp_second = from_neighbour(second, "y", 1)
    ym_first = from_neighbour(first, "y", -1)
    xa_yp = from_neighbour(yp_first, "x", 1)
    xb_ym = from_neighbour(ym_second, "x", -1)
    pooled = pooled / prompt_tally[0].astype(f32)
    normed = pooled * lax.rsqrt(jnp.mean(pooled * pooled) + 1e-06)
    cond = jax.nn.silu(normed).astype(bf16).reshape(encoded)
    local = jnp.dot(adaptive_norm_weights, cond, preferred_element_type=f32)
    columns = local.shape[0]
    rows = -(-columns // LANES)
    local = jnp.pad(local, (0, rows * LANES - columns)).reshape(rows, LANES)
    line = exchange(local, LINE)
    mine = exchange(after(waiting, line), LINE)
    halves = [block[part] for block in (yp_first, ym_second) for part in (slice(middle), slice(middle, None))]

    line, mine, halves, yp_second, ym_first, xa_yp, xb_ym = together(
        (line, mine, halves, yp_second, ym_first, xa_yp, xb_ym)
    )
    y2 = [from_neighbour(half, "y", 1 if i < 2 else -1) for i, half in enumerate(halves)]
    xa_ym = from_neighbour(ym_first, "x", 1)
    xb_yp = from_neighbour(yp_second, "x", -1)
    theirs = lax.ppermute(mine, "xh", [(0, 1), (1, 0)])
    modes = exchange(line, PLANE)
    modes = modes.reshape(-1, rows * LANES)[:, :columns].reshape(3, -1)
    xa_yp_down = xa_yp[middle:]
    xb_ym_down = xb_ym[middle:]

    y2, xa_ym, xb_yp, xa_yp_down, xb_ym_down, modes = together(
        (y2, xa_ym, xb_yp, xa_yp_down, xb_ym_down, modes)
    )
    xa_y2_up = from_neighbour(y2[0], "x", 1)
    xb_y2_up = from_neighbour(y2[2], "x", -1)
    xa_y2_down = from_neighbour(xa_yp_down, "y", 1)
    xb_y2_down = from_neighbour(xb_ym_down, "y", -1)

    whole = [
        first, second, xa, xb, yp_first, ym_second, yp_second, ym_first, xa_yp, xb_ym, xa_ym, xb_yp
    ]
    count = len(whole)
    total = (count + 4) * middle
    main = (total - 1) // STEP * STEP
    cut = main - (count + 1) * middle
    plan = [
        (i, which * middle, middle, which, i * middle) for i in range(count) for which in (0, 1)
    ]
    plan += [(count + which, 0, middle, which, count * middle) for which in (0, 1)]
    plan += [(count + 2 + which, 0, cut, which, main - cut) for which in (0, 1)]
    up_rows, down_rows = place(plan, whole + y2, main)
    upper = lax.axis_index("xh") == 1
    gathered = jnp.stack([jnp.where(upper, theirs, mine), jnp.where(upper, mine, theirs)])
    plan = [(which, cut, middle - cut, which, 0) for which in (0, 1)]
    plan += [
        (2 + 2 * which + i, 0, middle, which, (1 + i) * middle - cut)
        for which in (0, 1)
        for i in (0, 1)
    ]
    ends = [y2[2], y2[3], xa_y2_up, xb_y2_up, xa_y2_down, xb_y2_down]
    up_end, down_end = place(plan, ends, total - main)
    return modes, gathered, entering, (up_rows, down_rows, up_end, down_end)


def per_device(
    travelling_inputs,
    travelling_region,
    arriving_tiles,
    arriving_region,
    prompt_embeddings,
    prompt_tally,
    adaptive_norm_weights,
    expansion_weights,
    contraction_weights,
):
    section_id = lax.axis_index(SECTION)
    is_first = section_id == 0
    tokens, breadth = travelling_inputs.shape[1:]

    def with_mask(values, region):
        column = jnp.broadcast_to(region.astype(bf16)[:, None], (tokens, LANES))
        return jnp.concatenate([values, column], axis=1)

    arriving = with_mask(arriving_tiles[0], arriving_region[0])
    waiting = with_mask(travelling_inputs[0], travelling_region[0])
    last = SECTIONS - 1
    mod, gathered, entering, weights = set_out(
        expansion_weights[0],
        contraction_weights[0],
        prompt_embeddings,
        prompt_tally,
        adaptive_norm_weights[0],
        travelling_inputs[0],
        arriving,
    )
    is_third = section_id == 2
    gathered, waiting, gate, entering, is_first, is_third = lax.optimization_barrier(
        (gathered, waiting, mod[2:], entering, is_first, is_third)
    )
    moves = []
    for tick in range(SECTIONS):
        if tick:
            gathered = exchange(waiting[:, :breadth], GROUP)
        partial = layer(gathered.reshape(GROUP_SIZE * tokens, breadth), mod, *weights)
        parts = lax.all_to_all(partial.reshape(GROUP_SIZE, tokens, breadth), GROUP, 0, 0)
        if tick == last:
            third = between_sections(after(produced, parts), [(last, 2, 1)])
        produced = close(parts, waiting, gate)
        if tick < last:
            edges = [(0, 1, 0), (1, 2, 1), (2, 3, 0)]
            if tick < 2:
                edges.append((last, 0, 0))
        else:
            edges = [(0, 1, 0), (1, 2, 0), (2, 3, 1)]
        moves.append(between_sections(produced, edges))
        waiting = jnp.where(is_first, entering[tick], moves[tick])
    sent = jnp.where(is_first, moves[1], produced)
    second = between_sections(sent, [(0, 1, 0), (last, last, 1)])
    done = jnp.where(is_first, moves[0], jnp.where(is_third, third, second))
    return done[None, :, :breadth], waiting[None, :, :breadth]


def solution(mesh):
    fine = Mesh(mesh.devices.reshape(tuple(SIZES.values())), tuple(SIZES))
    placed = (
        P(SECTION, TP, None),
        P(SECTION, TP),
        P(SECTION, TP, None),
        P(SECTION, TP),
        P(SECTION + TP, None),
        P(),
        P(SECTION, TP, None),
        P(SECTION, TP, None),
        P(SECTION, TP, None),
    )
    return jax.shard_map(
        per_device,
        mesh=fine,
        in_specs=placed,
        out_specs=(P(SECTION, TP, None), P(SECTION, TP, None)),
        check_vma=False,
    )
```

```python
import functools

import jax
import jax.numpy as jnp
import numpy as np
from jax import lax
from jax.experimental import pallas as pl
from jax.experimental.pallas import tpu as pltpu
from jax.sharding import Mesh, PartitionSpec as P

f32 = jnp.float32
bf16 = jnp.bfloat16

SIZES = {"zh": 2, "core": 2, "xh": 2, "xl": 2, "yh": 2, "yl": 2, "zc": 2, "zf": 2}
SECTION = ("zh", "core")
TP = ("xh", "xl", "yh", "yl", "zc", "zf")
PLANE = ("xh", "xl", "yh", "yl")
LINE = ("zc", "zf")
GROUP = ("xh",) + LINE
GROUP_SIZE = 8
SECTIONS = 4
LANES = 128
STEP = 256


def from_neighbour(block, axis, distance):
    route = [((i + distance) % 4, i) for i in range(4)]
    return lax.ppermute(block, (axis + "h", axis + "l"), route)


def between_sections(block, edges):
    route = [
        (2 * start + half, 2 * end + (half ^ flip)) for start, end, flip in edges for half in (0, 1)
    ]
    return lax.ppermute(block, SECTION + ("zc",), route)


def after(value, *earlier):
    return lax.optimization_barrier((value,) + earlier)[0]


def exchange(block, axes):
    count = int(np.prod([SIZES[a] for a in axes]))
    copies = jnp.broadcast_to(block[None], (count,) + block.shape)
    return lax.all_to_all(copies, axes, 0, 0)


def modulate(x_ref, mod_ref, inputs):
    values = x_ref[...].astype(f32)
    center = jnp.mean(values, axis=1, keepdims=True)
    moved = values - center
    spread = jnp.mean(moved * moved, axis=1, keepdims=True)
    inputs[...] = (
        moved * lax.rsqrt(spread + 1e-06) * (1.0 + mod_ref[1:2]) + mod_ref[0:1]
    ).astype(bf16)


def layer_kernel(x_ref, mod_ref, up, down, up_end, down_end, out_ref, inputs, hidden):
    modulate(x_ref, mod_ref, inputs)
    main = up.shape[0]
    total = main + up_end.shape[0]
    for at in range(0, total, STEP):
        rows = up[at : at + STEP] if at < main else up_end[at - main : at - main + STEP]
        raised = lax.dot_general(
            inputs[...], rows, (((1,), (1,)), ((), ())), preferred_element_type=f32
        )
        hidden[:, at : at + STEP] = jax.nn.gelu(raised, approximate=True).astype(bf16)
    for at in range(0, out_ref.shape[1], STEP):
        columns = slice(at, at + STEP)
        result = jnp.dot(hidden[:, :main], down[:, columns], preferred_element_type=f32)
        result += jnp.dot(hidden[:, main:], down_end[:, columns], preferred_element_type=f32)
        out_ref[:, columns] = result.astype(bf16)


def layer(tokens, mod, up, down, up_end, down_end):
    rows, breadth = tokens.shape
    total = up.shape[0] + up_end.shape[0]
    whole = pl.BlockSpec(memory_space=pltpu.VMEM)
    return pl.pallas_call(
        layer_kernel,
        out_shape=jax.ShapeDtypeStruct((rows, breadth), bf16),
        in_specs=[whole] * 6,
        out_specs=whole,
        scratch_shapes=[
            pltpu.VMEM((rows, breadth), bf16),
            pltpu.VMEM((rows, total), bf16),
        ],
        compiler_params=pltpu.CompilerParams(vmem_limit_bytes=24 * 1024 * 1024),
        cost_estimate=pl.CostEstimate(
            flops=4 * rows * total * breadth,
            bytes_accessed=4 * total * breadth + 4 * rows * breadth,
            transcendentals=rows * total,
        ),
    )(tokens, mod, up, down, up_end, down_end)


def place_kernel(plan, *refs):
    sem = refs[-1]
    outs = refs[-3:-1]
    copies = []
    for piece, first, rows, which, at in plan:
        copies.append(
            pltpu.make_async_copy(
                refs[piece].at[pl.ds(first, rows)],
                outs[which].at[pl.ds(at, rows)],
                sem.at[len(copies)],
            )
        )
    for copy in copies:
        copy.start()
    for copy in copies:
        copy.wait()


def place(plan, pieces, total):
    breadth = pieces[0].shape[1]
    whole = pl.BlockSpec(memory_space=pltpu.VMEM)
    return pl.pallas_call(
        functools.partial(place_kernel, plan),
        out_shape=[jax.ShapeDtypeStruct((total, breadth), bf16)] * 2,
        in_specs=[pl.BlockSpec(memory_space=pl.ANY)] * len(pieces),
        out_specs=[whole] * 2,
        scratch_shapes=[pltpu.SemaphoreType.DMA((len(plan),))],
        compiler_params=pltpu.CompilerParams(vmem_limit_bytes=20 * 1024 * 1024),
        cost_estimate=pl.CostEstimate(
            flops=0, bytes_accessed=8 * total * breadth, transcendentals=0
        ),
    )(*pieces)


def close_kernel(parts_ref, waiting_ref, gate_ref, out_ref):
    breadth = parts_ref.shape[2]
    result = parts_ref[0].astype(f32)
    for i in range(1, parts_ref.shape[0]):
        result += parts_ref[i].astype(f32)
    mask = waiting_ref[:, breadth:]
    kept = mask[:, :1].astype(f32)
    values = waiting_ref[:, :breadth].astype(f32)
    out_ref[:, :breadth] = (values + kept * gate_ref[...] * result).astype(bf16)
    out_ref[:, breadth:] = mask


def close(parts, waiting, gate):
    whole = pl.BlockSpec(memory_space=pltpu.VMEM)
    return pl.pallas_call(
        close_kernel,
        out_shape=jax.ShapeDtypeStruct(waiting.shape, waiting.dtype),
        in_specs=[whole] * 3,
        out_specs=whole,
        compiler_params=pltpu.CompilerParams(vmem_limit_bytes=4 * 1024 * 1024),
        cost_estimate=pl.CostEstimate(
            flops=parts.size, bytes_accessed=2 * parts.size, transcendentals=0
        ),
    )(parts, waiting, gate)


def set_out(up, down, prompt_embeddings, prompt_tally, adaptive_norm_weights, waiting, arriving):
    together = lax.optimization_barrier
    middle = up.shape[0] // 2
    first = jnp.concatenate([up[:middle], down[:middle]], axis=0)
    second = jnp.concatenate([up[middle:], down[middle:]], axis=0)
    count_rows, encoded = prompt_embeddings.shape
    first_row = lax.axis_index(SECTION + TP) * count_rows
    keep = (first_row + lax.iota(jnp.int32, count_rows) < prompt_tally[0]).astype(bf16)
    partial = jnp.dot(keep[None, :], prompt_embeddings, preferred_element_type=f32)
    partial = partial.reshape(encoded // LANES, LANES)

    first, second, partial = together((first, second, partial))
    yp_first = from_neighbour(first, "y", 1)
    ym_second = from_neighbour(second, "y", -1)
    xa = from_neighbour(first, "x", 1)
    xb = from_neighbour(second, "x", -1)
    partial = jnp.sum(exchange(partial, SECTION + LINE), axis=0)
    entering = exchange(after(arriving, partial), SECTION)

    first, second, yp_first, ym_second, xa, xb, partial, entering = together(
        (first, second, yp_first, ym_second, xa, xb, partial, entering)
    )
    pooled = jnp.sum(exchange(partial, PLANE), axis=0)
    yp_second = from_neighbour(second, "y", 1)
    ym_first = from_neighbour(first, "y", -1)
    xa_yp = from_neighbour(yp_first, "x", 1)
    xb_ym = from_neighbour(ym_second, "x", -1)
    pooled = pooled / prompt_tally[0].astype(f32)
    normed = pooled * lax.rsqrt(jnp.mean(pooled * pooled) + 1e-06)
    cond = jax.nn.silu(normed).astype(bf16).reshape(encoded)
    local = jnp.dot(adaptive_norm_weights, cond, preferred_element_type=f32)
    columns = local.shape[0]
    rows = -(-columns // LANES)
    local = jnp.pad(local, (0, rows * LANES - columns)).reshape(rows, LANES)
    line = exchange(local, LINE)
    mine = exchange(after(waiting, line), LINE)
    halves = [block[part] for block in (yp_first, ym_second) for part in (slice(middle), slice(middle, None))]

    line, mine, halves, yp_second, ym_first, xa_yp, xb_ym = together(
        (line, mine, halves, yp_second, ym_first, xa_yp, xb_ym)
    )
    y2 = [from_neighbour(half, "y", 1 if i < 2 else -1) for i, half in enumerate(halves)]
    xa_ym = from_neighbour(ym_first, "x", 1)
    xb_yp = from_neighbour(yp_second, "x", -1)
    theirs = lax.ppermute(mine, "xh", [(0, 1), (1, 0)])
    modes = exchange(line, PLANE)
    modes = modes.reshape(-1, rows * LANES)[:, :columns].reshape(3, -1)
    xa_yp_down = xa_yp[middle:]
    xb_ym_down = xb_ym[middle:]

    y2, xa_ym, xb_yp, xa_yp_down, xb_ym_down, modes = together(
        (y2, xa_ym, xb_yp, xa_yp_down, xb_ym_down, modes)
    )
    xa_y2_up = from_neighbour(y2[0], "x", 1)
    xb_y2_up = from_neighbour(y2[2], "x", -1)
    xa_y2_down = from_neighbour(xa_yp_down, "y", 1)
    xb_y2_down = from_neighbour(xb_ym_down, "y", -1)

    whole = [
        first, second, xa, xb, yp_first, ym_second, yp_second, ym_first, xa_yp, xb_ym, xa_ym, xb_yp
    ]
    count = len(whole)
    total = (count + 4) * middle
    main = (total - 1) // STEP * STEP
    cut = main - (count + 1) * middle
    plan = [
        (i, which * middle, middle, which, i * middle) for i in range(count) for which in (0, 1)
    ]
    plan += [(count + which, 0, middle, which, count * middle) for which in (0, 1)]
    plan += [(count + 2 + which, 0, cut, which, main - cut) for which in (0, 1)]
    up_rows, down_rows = place(plan, whole + y2, main)
    upper = lax.axis_index("xh") == 1
    gathered = jnp.stack([jnp.where(upper, theirs, mine), jnp.where(upper, mine, theirs)])
    plan = [(which, cut, middle - cut, which, 0) for which in (0, 1)]
    plan += [
        (2 + 2 * which + i, 0, middle, which, (1 + i) * middle - cut)
        for which in (0, 1)
        for i in (0, 1)
    ]
    ends = [y2[2], y2[3], xa_y2_up, xb_y2_up, xa_y2_down, xb_y2_down]
    up_end, down_end = place(plan, ends, total - main)
    return modes, gathered, entering, (up_rows, down_rows, up_end, down_end)


def per_device(
    travelling_inputs,
    travelling_region,
    arriving_tiles,
    arriving_region,
    prompt_embeddings,
    prompt_tally,
    adaptive_norm_weights,
    expansion_weights,
    contraction_weights,
):
    section_id = lax.axis_index(SECTION)
    is_first = section_id == 0
    tokens, breadth = travelling_inputs.shape[1:]

    def with_mask(values, region):
        column = jnp.broadcast_to(region.astype(bf16)[:, None], (tokens, LANES))
        return jnp.concatenate([values, column], axis=1)

    arriving = with_mask(arriving_tiles[0], arriving_region[0])
    waiting = with_mask(travelling_inputs[0], travelling_region[0])
    last = SECTIONS - 1
    mod, gathered, entering, weights = set_out(
        expansion_weights[0],
        contraction_weights[0],
        prompt_embeddings,
        prompt_tally,
        adaptive_norm_weights[0],
        travelling_inputs[0],
        arriving,
    )
    is_third = section_id == 2
    entering = [entering[section] for section in range(SECTIONS)]
    gathered, waiting, gate, entering, is_first, is_third = lax.optimization_barrier(
        (gathered, waiting, mod[2:], entering, is_first, is_third)
    )
    moves = []
    for tick in range(SECTIONS):
        if tick:
            gathered = exchange(waiting[:, :breadth], GROUP)
        partial = layer(gathered.reshape(GROUP_SIZE * tokens, breadth), mod, *weights)
        parts = lax.all_to_all(partial.reshape(GROUP_SIZE, tokens, breadth), GROUP, 0, 0)
        if tick == last:
            third = between_sections(after(produced, parts), [(last, 2, 1)])
        produced = close(parts, waiting, gate)
        if tick < last:
            edges = [(0, 1, 0), (1, 2, 1), (2, 3, 0)]
            if tick < 2:
                edges.append((last, 0, 0))
        else:
            edges = [(0, 1, 0), (1, 2, 0), (2, 3, 1)]
        moves.append(between_sections(produced, edges))
        waiting = jnp.where(is_first, entering[tick], moves[tick])
    sent = jnp.where(is_first, moves[1], produced)
    second = between_sections(sent, [(0, 1, 0), (last, last, 1)])
    done = jnp.where(is_first, moves[0], jnp.where(is_third, third, second))
    return done[None, :, :breadth], waiting[None, :, :breadth]


def solution(mesh):
    fine = Mesh(mesh.devices.reshape(tuple(SIZES.values())), tuple(SIZES))
    placed = (
        P(SECTION, TP, None),
        P(SECTION, TP),
        P(SECTION, TP, None),
        P(SECTION, TP),
        P(SECTION + TP, None),
        P(),
        P(SECTION, TP, None),
        P(SECTION, TP, None),
        P(SECTION, TP, None),
    )
    return jax.shard_map(
        per_device,
        mesh=fine,
        in_specs=placed,
        out_specs=(P(SECTION, TP, None), P(SECTION, TP, None)),
        check_vma=False,
    )
```

```python
import functools

import jax
import jax.numpy as jnp
import numpy as np
from jax import lax
from jax.experimental import pallas as pl
from jax.experimental.pallas import tpu as pltpu
from jax.sharding import Mesh, PartitionSpec as P

f32 = jnp.float32
bf16 = jnp.bfloat16

SIZES = {"zh": 2, "core": 2, "xh": 2, "xl": 2, "yh": 2, "yl": 2, "zc": 2, "zf": 2}
SECTION = ("zh", "core")
TP = ("xh", "xl", "yh", "yl", "zc", "zf")
PLANE = ("xh", "xl", "yh", "yl")
LINE = ("zc", "zf")
GROUP = ("xh",) + LINE
GROUP_SIZE = 8
SECTIONS = 4
LANES = 128
STEP = 256


def from_neighbour(block, axis, distance):
    route = [((i + distance) % 4, i) for i in range(4)]
    return lax.ppermute(block, (axis + "h", axis + "l"), route)


def between_sections(block, edges):
    route = [
        (2 * start + half, 2 * end + (half ^ flip)) for start, end, flip in edges for half in (0, 1)
    ]
    return lax.ppermute(block, SECTION + ("zc",), route)


def after(value, *earlier):
    return lax.optimization_barrier((value,) + earlier)[0]


def exchange(block, axes):
    count = int(np.prod([SIZES[a] for a in axes]))
    copies = jnp.broadcast_to(block[None], (count,) + block.shape)
    return lax.all_to_all(copies, axes, 0, 0)


def modulate(x_ref, mod_ref, inputs):
    values = x_ref[...].astype(f32)
    center = jnp.mean(values, axis=1, keepdims=True)
    moved = values - center
    spread = jnp.mean(moved * moved, axis=1, keepdims=True)
    inputs[...] = (
        moved * lax.rsqrt(spread + 1e-06) * (1.0 + mod_ref[1:2]) + mod_ref[0:1]
    ).astype(bf16)


def layer_kernel(x_ref, mod_ref, up, down, up_end, down_end, out_ref, inputs, hidden):
    modulate(x_ref, mod_ref, inputs)
    main = up.shape[0]
    total = main + up_end.shape[0]
    for at in range(0, total, STEP):
        rows = up[at : at + STEP] if at < main else up_end[at - main : at - main + STEP]
        raised = lax.dot_general(
            inputs[...], rows, (((1,), (1,)), ((), ())), preferred_element_type=f32
        )
        hidden[:, at : at + STEP] = jax.nn.gelu(raised, approximate=True).astype(bf16)
    for at in range(0, out_ref.shape[1], STEP):
        columns = slice(at, at + STEP)
        result = jnp.dot(hidden[:, :main], down[:, columns], preferred_element_type=f32)
        result += jnp.dot(hidden[:, main:], down_end[:, columns], preferred_element_type=f32)
        out_ref[:, columns] = result.astype(bf16)


def layer(tokens, mod, up, down, up_end, down_end):
    rows, breadth = tokens.shape
    total = up.shape[0] + up_end.shape[0]
    whole = pl.BlockSpec(memory_space=pltpu.VMEM)
    return pl.pallas_call(
        layer_kernel,
        out_shape=jax.ShapeDtypeStruct((rows, breadth), bf16),
        in_specs=[whole] * 6,
        out_specs=whole,
        scratch_shapes=[
            pltpu.VMEM((rows, breadth), bf16),
            pltpu.VMEM((rows, total), bf16),
        ],
        compiler_params=pltpu.CompilerParams(vmem_limit_bytes=24 * 1024 * 1024),
        cost_estimate=pl.CostEstimate(
            flops=4 * rows * total * breadth,
            bytes_accessed=4 * total * breadth + 4 * rows * breadth,
            transcendentals=rows * total,
        ),
    )(tokens, mod, up, down, up_end, down_end)


def place_kernel(plan, *refs):
    sem = refs[-1]
    outs = refs[-3:-1]
    copies = []
    for piece, first, rows, which, at in plan:
        copies.append(
            pltpu.make_async_copy(
                refs[piece].at[pl.ds(first, rows)],
                outs[which].at[pl.ds(at, rows)],
                sem.at[len(copies)],
            )
        )
    for copy in copies:
        copy.start()
    for copy in copies:
        copy.wait()


def place(plan, pieces, total):
    breadth = pieces[0].shape[1]
    whole = pl.BlockSpec(memory_space=pltpu.VMEM)
    return pl.pallas_call(
        functools.partial(place_kernel, plan),
        out_shape=[jax.ShapeDtypeStruct((total, breadth), bf16)] * 2,
        in_specs=[pl.BlockSpec(memory_space=pl.ANY)] * len(pieces),
        out_specs=[whole] * 2,
        scratch_shapes=[pltpu.SemaphoreType.DMA((len(plan),))],
        compiler_params=pltpu.CompilerParams(vmem_limit_bytes=20 * 1024 * 1024),
        cost_estimate=pl.CostEstimate(
            flops=0, bytes_accessed=8 * total * breadth, transcendentals=0
        ),
    )(*pieces)


def close_kernel(parts_ref, waiting_ref, gate_ref, out_ref):
    breadth = parts_ref.shape[2]
    result = parts_ref[0].astype(f32)
    for i in range(1, parts_ref.shape[0]):
        result += parts_ref[i].astype(f32)
    mask = waiting_ref[:, breadth:]
    kept = mask[:, :1].astype(f32)
    values = waiting_ref[:, :breadth].astype(f32)
    out_ref[:, :breadth] = (values + kept * gate_ref[...] * result).astype(bf16)
    out_ref[:, breadth:] = mask


def close(parts, waiting, gate):
    whole = pl.BlockSpec(memory_space=pltpu.VMEM)
    return pl.pallas_call(
        close_kernel,
        out_shape=jax.ShapeDtypeStruct(waiting.shape, waiting.dtype),
        in_specs=[whole] * 3,
        out_specs=whole,
        compiler_params=pltpu.CompilerParams(vmem_limit_bytes=4 * 1024 * 1024),
        cost_estimate=pl.CostEstimate(
            flops=parts.size, bytes_accessed=2 * parts.size, transcendentals=0
        ),
    )(parts, waiting, gate)


def set_out(up, down, prompt_embeddings, prompt_tally, adaptive_norm_weights, waiting, arriving):
    together = lax.optimization_barrier
    middle = up.shape[0] // 2
    first = jnp.concatenate([up[:middle], down[:middle]], axis=0)
    second = jnp.concatenate([up[middle:], down[middle:]], axis=0)
    count_rows, encoded = prompt_embeddings.shape
    first_row = lax.axis_index(SECTION + TP) * count_rows
    keep = (first_row + lax.iota(jnp.int32, count_rows) < prompt_tally[0]).astype(bf16)
    partial = jnp.dot(keep[None, :], prompt_embeddings, preferred_element_type=f32)
    partial = partial.reshape(encoded // LANES, LANES)

    first, second, partial = together((first, second, partial))
    yp_first = from_neighbour(first, "y", 1)
    ym_second = from_neighbour(second, "y", -1)
    xa = from_neighbour(first, "x", 1)
    xb = from_neighbour(second, "x", -1)
    partial = jnp.sum(exchange(partial, SECTION + LINE), axis=0)
    entering = exchange(after(arriving, partial), SECTION)

    first, second, yp_first, ym_second, xa, xb, partial, entering = together(
        (first, second, yp_first, ym_second, xa, xb, partial, entering)
    )
    pooled = jnp.sum(exchange(partial, PLANE), axis=0)
    yp_second = from_neighbour(second, "y", 1)
    ym_first = from_neighbour(first, "y", -1)
    xa_yp = from_neighbour(yp_first, "x", 1)
    xb_ym = from_neighbour(ym_second, "x", -1)
    pooled = pooled / prompt_tally[0].astype(f32)
    normed = pooled * lax.rsqrt(jnp.mean(pooled * pooled) + 1e-06)
    cond = jax.nn.silu(normed).astype(bf16).reshape(encoded)
    local = jnp.dot(adaptive_norm_weights, cond, preferred_element_type=f32)
    columns = local.shape[0]
    rows = -(-columns // LANES)
    local = jnp.pad(local, (0, rows * LANES - columns)).reshape(rows, LANES)
    line = exchange(local, LINE)
    mine = exchange(after(waiting, line), LINE)
    halves = [block[part] for block in (yp_first, ym_second) for part in (slice(middle), slice(middle, None))]

    line, mine, halves, yp_second, ym_first, xa_yp, xb_ym = together(
        (line, mine, halves, yp_second, ym_first, xa_yp, xb_ym)
    )
    y2 = [from_neighbour(halves[0], "y", 1), None, from_neighbour(halves[2], "y", -1), None]
    xa_ym = from_neighbour(ym_first, "x", 1)
    xb_yp = from_neighbour(yp_second, "x", -1)
    halves, y2[0], y2[2] = together((halves, y2[0], y2[2]))
    y2[1] = from_neighbour(halves[1], "y", 1)
    y2[3] = from_neighbour(halves[3], "y", -1)
    theirs = lax.ppermute(mine, "xh", [(0, 1), (1, 0)])
    modes = exchange(line, PLANE)
    modes = modes.reshape(-1, rows * LANES)[:, :columns].reshape(3, -1)
    xa_yp_down = xa_yp[middle:]
    xb_ym_down = xb_ym[middle:]

    y2, xa_ym, xb_yp, xa_yp_down, xb_ym_down, modes = together(
        (y2, xa_ym, xb_yp, xa_yp_down, xb_ym_down, modes)
    )
    xa_y2_up = from_neighbour(y2[0], "x", 1)
    xb_y2_up = from_neighbour(y2[2], "x", -1)
    xa_y2_down = from_neighbour(xa_yp_down, "y", 1)
    xb_y2_down = from_neighbour(xb_ym_down, "y", -1)

    whole = [
        first, second, xa, xb, yp_first, ym_second, yp_second, ym_first, xa_yp, xb_ym, xa_ym, xb_yp
    ]
    count = len(whole)
    total = (count + 4) * middle
    main = (total - 1) // STEP * STEP
    cut = main - (count + 1) * middle
    plan = [
        (i, which * middle, middle, which, i * middle) for i in range(count) for which in (0, 1)
    ]
    plan += [(count + which, 0, middle, which, count * middle) for which in (0, 1)]
    plan += [(count + 2 + which, 0, cut, which, main - cut) for which in (0, 1)]
    up_rows, down_rows = place(plan, whole + y2, main)
    upper = lax.axis_index("xh") == 1
    gathered = jnp.stack([jnp.where(upper, theirs, mine), jnp.where(upper, mine, theirs)])
    plan = [(which, cut, middle - cut, which, 0) for which in (0, 1)]
    plan += [
        (2 + 2 * which + i, 0, middle, which, (1 + i) * middle - cut)
        for which in (0, 1)
        for i in (0, 1)
    ]
    ends = [y2[2], y2[3], xa_y2_up, xb_y2_up, xa_y2_down, xb_y2_down]
    up_end, down_end = place(plan, ends, total - main)
    return modes, gathered, entering, (up_rows, down_rows, up_end, down_end)


def per_device(
    travelling_inputs,
    travelling_region,
    arriving_tiles,
    arriving_region,
    prompt_embeddings,
    prompt_tally,
    adaptive_norm_weights,
    expansion_weights,
    contraction_weights,
):
    section_id = lax.axis_index(SECTION)
    is_first = section_id == 0
    tokens, breadth = travelling_inputs.shape[1:]

    def with_mask(values, region):
        column = jnp.broadcast_to(region.astype(bf16)[:, None], (tokens, LANES))
        return jnp.concatenate([values, column], axis=1)

    arriving = with_mask(arriving_tiles[0], arriving_region[0])
    waiting = with_mask(travelling_inputs[0], travelling_region[0])
    last = SECTIONS - 1
    mod, gathered, entering, weights = set_out(
        expansion_weights[0],
        contraction_weights[0],
        prompt_embeddings,
        prompt_tally,
        adaptive_norm_weights[0],
        travelling_inputs[0],
        arriving,
    )
    is_third = section_id == 2
    entering = [entering[section] for section in range(SECTIONS)]
    gathered, waiting, gate, entering, is_first, is_third = lax.optimization_barrier(
        (gathered, waiting, mod[2:], entering, is_first, is_third)
    )
    moves = []
    for tick in range(SECTIONS):
        if tick:
            gathered = exchange(waiting[:, :breadth], GROUP)
        partial = layer(gathered.reshape(GROUP_SIZE * tokens, breadth), mod, *weights)
        parts = lax.all_to_all(partial.reshape(GROUP_SIZE, tokens, breadth), GROUP, 0, 0)
        if tick == last:
            third = between_sections(after(produced, parts), [(last, 2, 1)])
        produced = close(parts, waiting, gate)
        if tick < last:
            edges = [(0, 1, 0), (1, 2, 1), (2, 3, 0)]
            if tick < 2:
                edges.append((last, 0, 0))
        else:
            edges = [(0, 1, 0), (1, 2, 0), (2, 3, 1)]
        moves.append(between_sections(produced, edges))
        waiting = jnp.where(is_first, entering[tick], moves[tick])
    sent = jnp.where(is_first, moves[1], produced)
    second = between_sections(sent, [(0, 1, 0), (last, last, 1)])
    done = jnp.where(is_first, moves[0], jnp.where(is_third, third, second))
    return done[None, :, :breadth], waiting[None, :, :breadth]


def solution(mesh):
    fine = Mesh(mesh.devices.reshape(tuple(SIZES.values())), tuple(SIZES))
    placed = (
        P(SECTION, TP, None),
        P(SECTION, TP),
        P(SECTION, TP, None),
        P(SECTION, TP),
        P(SECTION + TP, None),
        P(),
        P(SECTION, TP, None),
        P(SECTION, TP, None),
        P(SECTION, TP, None),
    )
    return jax.shard_map(
        per_device,
        mesh=fine,
        in_specs=placed,
        out_specs=(P(SECTION, TP, None), P(SECTION, TP, None)),
        check_vma=False,
    )
```

```python
import functools

import jax
import jax.numpy as jnp
import numpy as np
from jax import lax
from jax.experimental import pallas as pl
from jax.experimental.pallas import tpu as pltpu
from jax.sharding import Mesh, PartitionSpec as P

f32 = jnp.float32
bf16 = jnp.bfloat16

SIZES = {"zh": 2, "core": 2, "xh": 2, "xl": 2, "yh": 2, "yl": 2, "zc": 2, "zf": 2}
SECTION = ("zh", "core")
TP = ("xh", "xl", "yh", "yl", "zc", "zf")
PLANE = ("xh", "xl", "yh", "yl")
LINE = ("zc", "zf")
GROUP = ("xh",) + LINE
GROUP_SIZE = 8
SECTIONS = 4
LANES = 128
STEP = 256


def from_neighbour(block, axis, distance):
    route = [((i + distance) % 4, i) for i in range(4)]
    return lax.ppermute(block, (axis + "h", axis + "l"), route)


def between_sections(block, edges):
    route = [
        (2 * start + half, 2 * end + (half ^ flip)) for start, end, flip in edges for half in (0, 1)
    ]
    return lax.ppermute(block, SECTION + ("zc",), route)


def after(value, *earlier):
    return lax.optimization_barrier((value,) + earlier)[0]


def exchange(block, axes):
    count = int(np.prod([SIZES[a] for a in axes]))
    copies = jnp.broadcast_to(block[None], (count,) + block.shape)
    return lax.all_to_all(copies, axes, 0, 0)


def modulate(x_ref, mod_ref, inputs):
    values = x_ref[...].astype(f32)
    center = jnp.mean(values, axis=1, keepdims=True)
    moved = values - center
    spread = jnp.mean(moved * moved, axis=1, keepdims=True)
    inputs[...] = (
        moved * lax.rsqrt(spread + 1e-06) * (1.0 + mod_ref[1:2]) + mod_ref[0:1]
    ).astype(bf16)


def layer_kernel(x_ref, mod_ref, up, down, up_end, down_end, out_ref, inputs, hidden):
    modulate(x_ref, mod_ref, inputs)
    main = up.shape[0]
    total = main + up_end.shape[0]
    for at in range(0, total, STEP):
        rows = up[at : at + STEP] if at < main else up_end[at - main : at - main + STEP]
        raised = lax.dot_general(
            inputs[...], rows, (((1,), (1,)), ((), ())), preferred_element_type=f32
        )
        hidden[:, at : at + STEP] = jax.nn.gelu(raised, approximate=True).astype(bf16)
    for at in range(0, out_ref.shape[1], STEP):
        columns = slice(at, at + STEP)
        result = jnp.dot(hidden[:, :main], down[:, columns], preferred_element_type=f32)
        result += jnp.dot(hidden[:, main:], down_end[:, columns], preferred_element_type=f32)
        out_ref[:, columns] = result.astype(bf16)


def layer(tokens, mod, up, down, up_end, down_end):
    rows, breadth = tokens.shape
    total = up.shape[0] + up_end.shape[0]
    whole = pl.BlockSpec(memory_space=pltpu.VMEM)
    return pl.pallas_call(
        layer_kernel,
        out_shape=jax.ShapeDtypeStruct((rows, breadth), bf16),
        in_specs=[whole] * 6,
        out_specs=whole,
        scratch_shapes=[
            pltpu.VMEM((rows, breadth), bf16),
            pltpu.VMEM((rows, total), bf16),
        ],
        compiler_params=pltpu.CompilerParams(vmem_limit_bytes=24 * 1024 * 1024),
        cost_estimate=pl.CostEstimate(
            flops=4 * rows * total * breadth,
            bytes_accessed=4 * total * breadth + 4 * rows * breadth,
            transcendentals=rows * total,
        ),
    )(tokens, mod, up, down, up_end, down_end)


def place_kernel(plan, *refs):
    sem = refs[-1]
    outs = refs[-3:-1]
    copies = []
    for piece, first, rows, which, at in plan:
        copies.append(
            pltpu.make_async_copy(
                refs[piece].at[pl.ds(first, rows)],
                outs[which].at[pl.ds(at, rows)],
                sem.at[len(copies)],
            )
        )
    for copy in copies:
        copy.start()
    for copy in copies:
        copy.wait()


def place(plan, pieces, total):
    breadth = pieces[0].shape[1]
    whole = pl.BlockSpec(memory_space=pltpu.VMEM)
    return pl.pallas_call(
        functools.partial(place_kernel, plan),
        out_shape=[jax.ShapeDtypeStruct((total, breadth), bf16)] * 2,
        in_specs=[pl.BlockSpec(memory_space=pl.ANY)] * len(pieces),
        out_specs=[whole] * 2,
        scratch_shapes=[pltpu.SemaphoreType.DMA((len(plan),))],
        compiler_params=pltpu.CompilerParams(vmem_limit_bytes=20 * 1024 * 1024),
        cost_estimate=pl.CostEstimate(
            flops=0, bytes_accessed=8 * total * breadth, transcendentals=0
        ),
    )(*pieces)


def close_kernel(parts_ref, waiting_ref, gate_ref, out_ref):
    breadth = parts_ref.shape[2]
    result = parts_ref[0].astype(f32)
    for i in range(1, parts_ref.shape[0]):
        result += parts_ref[i].astype(f32)
    mask = waiting_ref[:, breadth:]
    kept = mask[:, :1].astype(f32)
    values = waiting_ref[:, :breadth].astype(f32)
    out_ref[:, :breadth] = (values + kept * gate_ref[...] * result).astype(bf16)
    out_ref[:, breadth:] = mask


def close(parts, waiting, gate):
    whole = pl.BlockSpec(memory_space=pltpu.VMEM)
    return pl.pallas_call(
        close_kernel,
        out_shape=jax.ShapeDtypeStruct(waiting.shape, waiting.dtype),
        in_specs=[whole] * 3,
        out_specs=whole,
        compiler_params=pltpu.CompilerParams(vmem_limit_bytes=4 * 1024 * 1024),
        cost_estimate=pl.CostEstimate(
            flops=parts.size, bytes_accessed=2 * parts.size, transcendentals=0
        ),
    )(parts, waiting, gate)


def set_out(up, down, prompt_embeddings, prompt_tally, adaptive_norm_weights, waiting, arriving):
    together = lax.optimization_barrier
    middle = up.shape[0] // 2
    first = jnp.concatenate([up[:middle], down[:middle]], axis=0)
    second = jnp.concatenate([up[middle:], down[middle:]], axis=0)
    count_rows, encoded = prompt_embeddings.shape
    first_row = lax.axis_index(SECTION + TP) * count_rows
    keep = (first_row + lax.iota(jnp.int32, count_rows) < prompt_tally[0]).astype(bf16)
    partial = jnp.dot(keep[None, :], prompt_embeddings, preferred_element_type=f32)
    partial = partial.reshape(encoded // LANES, LANES)

    first, second, partial = together((first, second, partial))
    yp_first = from_neighbour(first, "y", 1)
    ym_second = from_neighbour(second, "y", -1)
    xa = from_neighbour(first, "x", 1)
    xb = from_neighbour(second, "x", -1)
    partial = jnp.sum(exchange(partial, SECTION + LINE), axis=0)
    entering = exchange(after(arriving, partial), SECTION)

    first, second, yp_first, ym_second, xa, xb, partial, entering = together(
        (first, second, yp_first, ym_second, xa, xb, partial, entering)
    )
    pooled = jnp.sum(exchange(partial, PLANE), axis=0)
    yp_second = from_neighbour(second, "y", 1)
    ym_first = from_neighbour(first, "y", -1)
    xa_yp = from_neighbour(yp_first, "x", 1)
    xb_ym = from_neighbour(ym_second, "x", -1)
    pooled = pooled / prompt_tally[0].astype(f32)
    normed = pooled * lax.rsqrt(jnp.mean(pooled * pooled) + 1e-06)
    cond = jax.nn.silu(normed).astype(bf16).reshape(encoded)
    local = jnp.dot(adaptive_norm_weights, cond, preferred_element_type=f32)
    columns = local.shape[0]
    rows = -(-columns // LANES)
    local = jnp.pad(local, (0, rows * LANES - columns)).reshape(rows, LANES)
    line = exchange(local, LINE)
    mine = exchange(after(waiting, line), LINE)
    halves = [block[part] for block in (yp_first, ym_second) for part in (slice(middle), slice(middle, None))]

    line, mine, halves, yp_second, ym_first, xa_yp, xb_ym = together(
        (line, mine, halves, yp_second, ym_first, xa_yp, xb_ym)
    )
    y2 = [from_neighbour(halves[0], "y", 1), None, from_neighbour(halves[2], "y", -1), None]
    xa_ym = from_neighbour(ym_first, "x", 1)
    xb_yp = from_neighbour(yp_second, "x", -1)
    halves, y2[0], y2[2] = together((halves, y2[0], y2[2]))
    y2[1] = from_neighbour(halves[1], "y", 1)
    y2[3] = from_neighbour(halves[3], "y", -1)
    theirs = lax.ppermute(mine, "xh", [(0, 1), (1, 0)])
    modes = exchange(line, PLANE)
    xa_yp_down = xa_yp[middle:]
    xb_ym_down = xb_ym[middle:]

    y2, xa_ym, xb_yp, xa_yp_down, xb_ym_down, modes = together(
        (y2, xa_ym, xb_yp, xa_yp_down, xb_ym_down, modes)
    )
    modes = modes.reshape(-1, rows * LANES)[:, :columns].reshape(3, -1)
    xa_y2_up = from_neighbour(y2[0], "x", 1)
    xb_y2_up = from_neighbour(y2[2], "x", -1)
    xa_y2_down = from_neighbour(xa_yp_down, "y", 1)
    xb_y2_down = from_neighbour(xb_ym_down, "y", -1)

    whole = [
        first, second, xa, xb, yp_first, ym_second, yp_second, ym_first, xa_yp, xb_ym, xa_ym, xb_yp
    ]
    count = len(whole)
    total = (count + 4) * middle
    main = (total - 1) // STEP * STEP
    cut = main - (count + 1) * middle
    plan = [
        (i, which * middle, middle, which, i * middle) for i in range(count) for which in (0, 1)
    ]
    plan += [(count + which, 0, middle, which, count * middle) for which in (0, 1)]
    plan += [(count + 2 + which, 0, cut, which, main - cut) for which in (0, 1)]
    up_rows, down_rows = place(plan, whole + y2, main)
    upper = lax.axis_index("xh") == 1
    gathered = jnp.stack([jnp.where(upper, theirs, mine), jnp.where(upper, mine, theirs)])
    plan = [(which, cut, middle - cut, which, 0) for which in (0, 1)]
    plan += [
        (2 + 2 * which + i, 0, middle, which, (1 + i) * middle - cut)
        for which in (0, 1)
        for i in (0, 1)
    ]
    ends = [y2[2], y2[3], xa_y2_up, xb_y2_up, xa_y2_down, xb_y2_down]
    up_end, down_end = place(plan, ends, total - main)
    return modes, gathered, entering, (up_rows, down_rows, up_end, down_end)


def per_device(
    travelling_inputs,
    travelling_region,
    arriving_tiles,
    arriving_region,
    prompt_embeddings,
    prompt_tally,
    adaptive_norm_weights,
    expansion_weights,
    contraction_weights,
):
    section_id = lax.axis_index(SECTION)
    is_first = section_id == 0
    tokens, breadth = travelling_inputs.shape[1:]

    def with_mask(values, region):
        column = jnp.broadcast_to(region.astype(bf16)[:, None], (tokens, LANES))
        return jnp.concatenate([values, column], axis=1)

    arriving = with_mask(arriving_tiles[0], arriving_region[0])
    waiting = with_mask(travelling_inputs[0], travelling_region[0])
    last = SECTIONS - 1
    mod, gathered, entering, weights = set_out(
        expansion_weights[0],
        contraction_weights[0],
        prompt_embeddings,
        prompt_tally,
        adaptive_norm_weights[0],
        travelling_inputs[0],
        arriving,
    )
    is_third = section_id == 2
    entering = [entering[section] for section in range(SECTIONS)]
    gathered, waiting, gate, entering, is_first, is_third = lax.optimization_barrier(
        (gathered, waiting, mod[2:], entering, is_first, is_third)
    )
    moves = []
    for tick in range(SECTIONS):
        if tick:
            gathered = exchange(waiting[:, :breadth], GROUP)
        partial = layer(gathered.reshape(GROUP_SIZE * tokens, breadth), mod, *weights)
        parts = lax.all_to_all(partial.reshape(GROUP_SIZE, tokens, breadth), GROUP, 0, 0)
        if tick == last:
            third = between_sections(after(produced, parts), [(last, 2, 1)])
        produced = close(parts, waiting, gate)
        if tick < last:
            edges = [(0, 1, 0), (1, 2, 1), (2, 3, 0)]
            if tick < 2:
                edges.append((last, 0, 0))
        else:
            edges = [(0, 1, 0), (1, 2, 0), (2, 3, 1)]
        moves.append(between_sections(produced, edges))
        waiting = jnp.where(is_first, entering[tick], moves[tick])
    sent = jnp.where(is_first, moves[1], produced)
    second = between_sections(sent, [(0, 1, 0), (last, last, 1)])
    done = jnp.where(is_first, moves[0], jnp.where(is_third, third, second))
    return done[None, :, :breadth], waiting[None, :, :breadth]


def solution(mesh):
    fine = Mesh(mesh.devices.reshape(tuple(SIZES.values())), tuple(SIZES))
    placed = (
        P(SECTION, TP, None),
        P(SECTION, TP),
        P(SECTION, TP, None),
        P(SECTION, TP),
        P(SECTION + TP, None),
        P(),
        P(SECTION, TP, None),
        P(SECTION, TP, None),
        P(SECTION, TP, None),
    )
    return jax.shard_map(
        per_device,
        mesh=fine,
        in_specs=placed,
        out_specs=(P(SECTION, TP, None), P(SECTION, TP, None)),
        check_vma=False,
    )
```

```python
import functools

import jax
import jax.numpy as jnp
import numpy as np
from jax import lax
from jax.experimental import pallas as pl
from jax.experimental.pallas import tpu as pltpu
from jax.sharding import Mesh, PartitionSpec as P

f32 = jnp.float32
bf16 = jnp.bfloat16

SIZES = {"zh": 2, "core": 2, "xh": 2, "xl": 2, "yh": 2, "yl": 2, "zc": 2, "zf": 2}
SECTION = ("zh", "core")
TP = ("xh", "xl", "yh", "yl", "zc", "zf")
PLANE = ("xh", "xl", "yh", "yl")
LINE = ("zc", "zf")
GROUP = ("xh",) + LINE
GROUP_SIZE = 8
SECTIONS = 4
LANES = 128
STEP = 256


def from_neighbour(block, axis, distance):
    route = [((i + distance) % 4, i) for i in range(4)]
    return lax.ppermute(block, (axis + "h", axis + "l"), route)


def between_sections(block, edges):
    route = [
        (2 * start + half, 2 * end + (half ^ flip)) for start, end, flip in edges for half in (0, 1)
    ]
    return lax.ppermute(block, SECTION + ("zc",), route)


def after(value, *earlier):
    return lax.optimization_barrier((value,) + earlier)[0]


def exchange(block, axes):
    count = int(np.prod([SIZES[a] for a in axes]))
    copies = jnp.broadcast_to(block[None], (count,) + block.shape)
    return lax.all_to_all(copies, axes, 0, 0)


def modulate(x_ref, mod_ref, inputs):
    values = x_ref[...].astype(f32)
    center = jnp.mean(values, axis=1, keepdims=True)
    moved = values - center
    spread = jnp.mean(moved * moved, axis=1, keepdims=True)
    inputs[...] = (
        moved * lax.rsqrt(spread + 1e-06) * (1.0 + mod_ref[1:2]) + mod_ref[0:1]
    ).astype(bf16)


def layer_kernel(x_ref, mod_ref, up, down, up_end, down_end, out_ref, inputs, hidden):
    modulate(x_ref, mod_ref, inputs)
    main = up.shape[0]
    total = main + up_end.shape[0]
    for at in range(0, total, STEP):
        rows = up[at : at + STEP] if at < main else up_end[at - main : at - main + STEP]
        raised = lax.dot_general(
            inputs[...], rows, (((1,), (1,)), ((), ())), preferred_element_type=f32
        )
        hidden[:, at : at + STEP] = jax.nn.gelu(raised, approximate=True).astype(bf16)
    for at in range(0, out_ref.shape[1], STEP):
        columns = slice(at, at + STEP)
        result = jnp.dot(hidden[:, :main], down[:, columns], preferred_element_type=f32)
        result += jnp.dot(hidden[:, main:], down_end[:, columns], preferred_element_type=f32)
        out_ref[:, columns] = result.astype(bf16)


def layer(tokens, mod, up, down, up_end, down_end):
    rows, breadth = tokens.shape
    total = up.shape[0] + up_end.shape[0]
    whole = pl.BlockSpec(memory_space=pltpu.VMEM)
    return pl.pallas_call(
        layer_kernel,
        out_shape=jax.ShapeDtypeStruct((rows, breadth), bf16),
        in_specs=[whole] * 6,
        out_specs=whole,
        scratch_shapes=[
            pltpu.VMEM((rows, breadth), bf16),
            pltpu.VMEM((rows, total), bf16),
        ],
        compiler_params=pltpu.CompilerParams(vmem_limit_bytes=24 * 1024 * 1024),
        cost_estimate=pl.CostEstimate(
            flops=4 * rows * total * breadth,
            bytes_accessed=4 * total * breadth + 4 * rows * breadth,
            transcendentals=rows * total,
        ),
    )(tokens, mod, up, down, up_end, down_end)


def place_kernel(plan, *refs):
    sem = refs[-1]
    outs = refs[-3:-1]
    copies = []
    for piece, first, rows, which, at in plan:
        copies.append(
            pltpu.make_async_copy(
                refs[piece].at[pl.ds(first, rows)],
                outs[which].at[pl.ds(at, rows)],
                sem.at[len(copies)],
            )
        )
    for copy in copies:
        copy.start()
    for copy in copies:
        copy.wait()


def place(plan, pieces, total):
    breadth = pieces[0].shape[1]
    whole = pl.BlockSpec(memory_space=pltpu.VMEM)
    return pl.pallas_call(
        functools.partial(place_kernel, plan),
        out_shape=[jax.ShapeDtypeStruct((total, breadth), bf16)] * 2,
        in_specs=[pl.BlockSpec(memory_space=pl.ANY)] * len(pieces),
        out_specs=[whole] * 2,
        scratch_shapes=[pltpu.SemaphoreType.DMA((len(plan),))],
        compiler_params=pltpu.CompilerParams(vmem_limit_bytes=20 * 1024 * 1024),
        cost_estimate=pl.CostEstimate(
            flops=0, bytes_accessed=8 * total * breadth, transcendentals=0
        ),
    )(*pieces)


def close_kernel(parts_ref, waiting_ref, gate_ref, out_ref):
    breadth = parts_ref.shape[2]
    result = parts_ref[0].astype(f32)
    for i in range(1, parts_ref.shape[0]):
        result += parts_ref[i].astype(f32)
    mask = waiting_ref[:, breadth:]
    kept = mask[:, :1].astype(f32)
    values = waiting_ref[:, :breadth].astype(f32)
    out_ref[:, :breadth] = (values + kept * gate_ref[...] * result).astype(bf16)
    out_ref[:, breadth:] = mask


def close(parts, waiting, gate):
    whole = pl.BlockSpec(memory_space=pltpu.VMEM)
    return pl.pallas_call(
        close_kernel,
        out_shape=jax.ShapeDtypeStruct(waiting.shape, waiting.dtype),
        in_specs=[whole] * 3,
        out_specs=whole,
        compiler_params=pltpu.CompilerParams(vmem_limit_bytes=4 * 1024 * 1024),
        cost_estimate=pl.CostEstimate(
            flops=parts.size, bytes_accessed=2 * parts.size, transcendentals=0
        ),
    )(parts, waiting, gate)


def set_out(up, down, prompt_embeddings, prompt_tally, adaptive_norm_weights, waiting, arriving):
    together = lax.optimization_barrier
    middle = up.shape[0] // 2
    first = jnp.concatenate([up[:middle], down[:middle]], axis=0)
    second = jnp.concatenate([up[middle:], down[middle:]], axis=0)
    count_rows, encoded = prompt_embeddings.shape
    first_row = lax.axis_index(SECTION + TP) * count_rows
    keep = (first_row + lax.iota(jnp.int32, count_rows) < prompt_tally[0]).astype(bf16)
    partial = jnp.dot(keep[None, :], prompt_embeddings, preferred_element_type=f32)
    partial = partial.reshape(encoded // LANES, LANES)

    first, second, partial = together((first, second, partial))
    yp_first = from_neighbour(first, "y", 1)
    ym_second = from_neighbour(second, "y", -1)
    xa = from_neighbour(first, "x", 1)
    xb = from_neighbour(second, "x", -1)
    partial = jnp.sum(exchange(partial, SECTION + LINE), axis=0)
    entering = exchange(after(arriving, partial), SECTION)

    first, second, yp_first, ym_second, xa, xb, partial, entering = together(
        (first, second, yp_first, ym_second, xa, xb, partial, entering)
    )
    pooled = jnp.sum(exchange(partial, PLANE), axis=0)
    yp_second = from_neighbour(second, "y", 1)
    ym_first = from_neighbour(first, "y", -1)
    xa_yp = from_neighbour(yp_first, "x", 1)
    xb_ym = from_neighbour(ym_second, "x", -1)
    pooled = pooled / prompt_tally[0].astype(f32)
    normed = pooled * lax.rsqrt(jnp.mean(pooled * pooled) + 1e-06)
    cond = jax.nn.silu(normed).astype(bf16).reshape(encoded)
    local = jnp.dot(adaptive_norm_weights, cond, preferred_element_type=f32)
    columns = local.shape[0]
    rows = -(-columns // LANES)
    local = jnp.pad(local, (0, rows * LANES - columns)).reshape(rows, LANES)
    line = exchange(local, LINE)
    mine = exchange(after(waiting, line), LINE)
    halves = [block[part] for block in (yp_first, ym_second) for part in (slice(middle), slice(middle, None))]

    line, mine, halves, yp_second, ym_first, xa_yp, xb_ym = together(
        (line, mine, halves, yp_second, ym_first, xa_yp, xb_ym)
    )
    y2 = [from_neighbour(halves[0], "y", 1), None, from_neighbour(halves[2], "y", -1), None]
    xa_ym = from_neighbour(ym_first, "x", 1)
    xb_yp = from_neighbour(yp_second, "x", -1)
    halves, y2[0], y2[2] = together((halves, y2[0], y2[2]))
    y2[1] = from_neighbour(halves[1], "y", 1)
    y2[3] = from_neighbour(halves[3], "y", -1)
    modes = exchange(line, PLANE)
    xa_yp_down = xa_yp[middle:]
    xb_ym_down = xb_ym[middle:]

    modes = modes.reshape(-1, rows * LANES)[:, :columns].reshape(3, -1)
    xa_y2_up = from_neighbour(y2[0], "x", 1)
    xb_y2_up = from_neighbour(y2[2], "x", -1)
    xa_y2_down = from_neighbour(xa_yp_down, "y", 1)
    xb_y2_down = from_neighbour(xb_ym_down, "y", -1)

    whole = [
        first, second, xa, xb, yp_first, ym_second, yp_second, ym_first, xa_yp, xb_ym, xa_ym, xb_yp
    ]
    count = len(whole)
    total = (count + 4) * middle
    main = (total - 1) // STEP * STEP
    cut = main - (count + 1) * middle
    plan = [
        (i, which * middle, middle, which, i * middle) for i in range(count) for which in (0, 1)
    ]
    plan += [(count + which, 0, middle, which, count * middle) for which in (0, 1)]
    plan += [(count + 2 + which, 0, cut, which, main - cut) for which in (0, 1)]
    up_rows, down_rows = place(plan, after(whole + y2, modes), main)
    theirs = lax.ppermute(after(mine, xa_ym, xb_yp), "xh", [(0, 1), (1, 0)])
    upper = lax.axis_index("xh") == 1
    gathered = jnp.stack([jnp.where(upper, theirs, mine), jnp.where(upper, mine, theirs)])
    plan = [(which, cut, middle - cut, which, 0) for which in (0, 1)]
    plan += [
        (2 + 2 * which + i, 0, middle, which, (1 + i) * middle - cut)
        for which in (0, 1)
        for i in (0, 1)
    ]
    ends = [y2[2], y2[3], xa_y2_up, xb_y2_up, xa_y2_down, xb_y2_down]
    up_end, down_end = place(plan, ends, total - main)
    return modes, gathered, entering, (up_rows, down_rows, up_end, down_end)


def per_device(
    travelling_inputs,
    travelling_region,
    arriving_tiles,
    arriving_region,
    prompt_embeddings,
    prompt_tally,
    adaptive_norm_weights,
    expansion_weights,
    contraction_weights,
):
    section_id = lax.axis_index(SECTION)
    is_first = section_id == 0
    tokens, breadth = travelling_inputs.shape[1:]

    def with_mask(values, region):
        column = jnp.broadcast_to(region.astype(bf16)[:, None], (tokens, LANES))
        return jnp.concatenate([values, column], axis=1)

    arriving = with_mask(arriving_tiles[0], arriving_region[0])
    waiting = with_mask(travelling_inputs[0], travelling_region[0])
    last = SECTIONS - 1
    mod, gathered, entering, weights = set_out(
        expansion_weights[0],
        contraction_weights[0],
        prompt_embeddings,
        prompt_tally,
        adaptive_norm_weights[0],
        travelling_inputs[0],
        arriving,
    )
    is_third = section_id == 2
    entering = [entering[section] for section in range(SECTIONS)]
    gathered, waiting, gate, entering, is_first, is_third = lax.optimization_barrier(
        (gathered, waiting, mod[2:], entering, is_first, is_third)
    )
    moves = []
    for tick in range(SECTIONS):
        if tick:
            gathered = exchange(waiting[:, :breadth], GROUP)
        partial = layer(gathered.reshape(GROUP_SIZE * tokens, breadth), mod, *weights)
        parts = lax.all_to_all(partial.reshape(GROUP_SIZE, tokens, breadth), GROUP, 0, 0)
        if tick == last:
            third = between_sections(after(produced, parts), [(last, 2, 1)])
        produced = close(parts, waiting, gate)
        if tick < last:
            edges = [(0, 1, 0), (1, 2, 1), (2, 3, 0)]
            if tick < 2:
                edges.append((last, 0, 0))
        else:
            edges = [(0, 1, 0), (1, 2, 0), (2, 3, 1)]
        moves.append(between_sections(produced, edges))
        waiting = jnp.where(is_first, entering[tick], moves[tick])
    sent = jnp.where(is_first, moves[1], produced)
    second = between_sections(sent, [(0, 1, 0), (last, last, 1)])
    done = jnp.where(is_first, moves[0], jnp.where(is_third, third, second))
    return done[None, :, :breadth], waiting[None, :, :breadth]


def solution(mesh):
    fine = Mesh(mesh.devices.reshape(tuple(SIZES.values())), tuple(SIZES))
    placed = (
        P(SECTION, TP, None),
        P(SECTION, TP),
        P(SECTION, TP, None),
        P(SECTION, TP),
        P(SECTION + TP, None),
        P(),
        P(SECTION, TP, None),
        P(SECTION, TP, None),
        P(SECTION, TP, None),
    )
    return jax.shard_map(
        per_device,
        mesh=fine,
        in_specs=placed,
        out_specs=(P(SECTION, TP, None), P(SECTION, TP, None)),
        check_vma=False,
    )
```

```python
import functools

import jax
import jax.numpy as jnp
import numpy as np
from jax import lax
from jax.experimental import pallas as pl
from jax.experimental.pallas import tpu as pltpu
from jax.sharding import Mesh, PartitionSpec as P

f32 = jnp.float32
bf16 = jnp.bfloat16

SIZES = {"zh": 2, "core": 2, "xh": 2, "xl": 2, "yh": 2, "yl": 2, "zc": 2, "zf": 2}
SECTION = ("zh", "core")
TP = ("xh", "xl", "yh", "yl", "zc", "zf")
PLANE = ("xh", "xl", "yh", "yl")
LINE = ("zc", "zf")
GROUP = ("xh",) + LINE
GROUP_SIZE = 8
SECTIONS = 4
LANES = 128
STEP = 256


def from_neighbour(block, axis, distance):
    route = [((i + distance) % 4, i) for i in range(4)]
    return lax.ppermute(block, (axis + "h", axis + "l"), route)


def between_sections(block, edges):
    route = [
        (2 * start + half, 2 * end + (half ^ flip)) for start, end, flip in edges for half in (0, 1)
    ]
    return lax.ppermute(block, SECTION + ("zc",), route)


def after(value, *earlier):
    return lax.optimization_barrier((value,) + earlier)[0]


def exchange(block, axes):
    count = int(np.prod([SIZES[a] for a in axes]))
    copies = jnp.broadcast_to(block[None], (count,) + block.shape)
    return lax.all_to_all(copies, axes, 0, 0)


def modulate(x_ref, mod_ref, inputs):
    values = x_ref[...].astype(f32)
    center = jnp.mean(values, axis=1, keepdims=True)
    moved = values - center
    spread = jnp.mean(moved * moved, axis=1, keepdims=True)
    inputs[...] = (
        moved * lax.rsqrt(spread + 1e-06) * (1.0 + mod_ref[1:2]) + mod_ref[0:1]
    ).astype(bf16)


def layer_kernel(x_ref, mod_ref, up, down, up_end, down_end, out_ref, inputs, hidden):
    modulate(x_ref, mod_ref, inputs)
    main = up.shape[0]
    total = main + up_end.shape[0]
    for at in range(0, total, STEP):
        rows = up[at : at + STEP] if at < main else up_end[at - main : at - main + STEP]
        raised = lax.dot_general(
            inputs[...], rows, (((1,), (1,)), ((), ())), preferred_element_type=f32
        )
        hidden[:, at : at + STEP] = jax.nn.gelu(raised, approximate=True).astype(bf16)
    for at in range(0, out_ref.shape[1], STEP):
        columns = slice(at, at + STEP)
        result = jnp.dot(hidden[:, :main], down[:, columns], preferred_element_type=f32)
        result += jnp.dot(hidden[:, main:], down_end[:, columns], preferred_element_type=f32)
        out_ref[:, columns] = result.astype(bf16)


def layer(tokens, mod, up, down, up_end, down_end):
    rows, breadth = tokens.shape
    total = up.shape[0] + up_end.shape[0]
    whole = pl.BlockSpec(memory_space=pltpu.VMEM)
    return pl.pallas_call(
        layer_kernel,
        out_shape=jax.ShapeDtypeStruct((rows, breadth), bf16),
        in_specs=[whole] * 6,
        out_specs=whole,
        scratch_shapes=[
            pltpu.VMEM((rows, breadth), bf16),
            pltpu.VMEM((rows, total), bf16),
        ],
        compiler_params=pltpu.CompilerParams(vmem_limit_bytes=24 * 1024 * 1024),
        cost_estimate=pl.CostEstimate(
            flops=4 * rows * total * breadth,
            bytes_accessed=4 * total * breadth + 4 * rows * breadth,
            transcendentals=rows * total,
        ),
    )(tokens, mod, up, down, up_end, down_end)


def place_kernel(plan, *refs):
    sem = refs[-1]
    outs = refs[-3:-1]
    copies = []
    for piece, first, rows, which, at in plan:
        copies.append(
            pltpu.make_async_copy(
                refs[piece].at[pl.ds(first, rows)],
                outs[which].at[pl.ds(at, rows)],
                sem.at[len(copies)],
            )
        )
    for copy in copies:
        copy.start()
    for copy in copies:
        copy.wait()


def place(plan, pieces, total):
    breadth = pieces[0].shape[1]
    whole = pl.BlockSpec(memory_space=pltpu.VMEM)
    return pl.pallas_call(
        functools.partial(place_kernel, plan),
        out_shape=[jax.ShapeDtypeStruct((total, breadth), bf16)] * 2,
        in_specs=[pl.BlockSpec(memory_space=pl.ANY)] * len(pieces),
        out_specs=[whole] * 2,
        scratch_shapes=[pltpu.SemaphoreType.DMA((len(plan),))],
        compiler_params=pltpu.CompilerParams(vmem_limit_bytes=20 * 1024 * 1024),
        cost_estimate=pl.CostEstimate(
            flops=0, bytes_accessed=8 * total * breadth, transcendentals=0
        ),
    )(*pieces)


def close_kernel(parts_ref, waiting_ref, gate_ref, out_ref):
    breadth = parts_ref.shape[2]
    result = parts_ref[0].astype(f32)
    for i in range(1, parts_ref.shape[0]):
        result += parts_ref[i].astype(f32)
    mask = waiting_ref[:, breadth:]
    kept = mask[:, :1].astype(f32)
    values = waiting_ref[:, :breadth].astype(f32)
    out_ref[:, :breadth] = (values + kept * gate_ref[...] * result).astype(bf16)
    out_ref[:, breadth:] = mask


def close(parts, waiting, gate):
    whole = pl.BlockSpec(memory_space=pltpu.VMEM)
    return pl.pallas_call(
        close_kernel,
        out_shape=jax.ShapeDtypeStruct(waiting.shape, waiting.dtype),
        in_specs=[whole] * 3,
        out_specs=whole,
        compiler_params=pltpu.CompilerParams(vmem_limit_bytes=4 * 1024 * 1024),
        cost_estimate=pl.CostEstimate(
            flops=parts.size, bytes_accessed=2 * parts.size, transcendentals=0
        ),
    )(parts, waiting, gate)


def set_out(up, down, prompt_embeddings, prompt_tally, adaptive_norm_weights, waiting, arriving):
    together = lax.optimization_barrier
    middle = up.shape[0] // 2
    first = jnp.concatenate([up[:middle], down[:middle]], axis=0)
    second = jnp.concatenate([up[middle:], down[middle:]], axis=0)
    count_rows, encoded = prompt_embeddings.shape
    first_row = lax.axis_index(SECTION + TP) * count_rows
    keep = (first_row + lax.iota(jnp.int32, count_rows) < prompt_tally[0]).astype(bf16)
    partial = jnp.dot(keep[None, :], prompt_embeddings, preferred_element_type=f32)
    partial = partial.reshape(encoded // LANES, LANES)

    first, second, partial = together((first, second, partial))
    yp_first = from_neighbour(first, "y", 1)
    ym_second = from_neighbour(second, "y", -1)
    xa = from_neighbour(first, "x", 1)
    xb = from_neighbour(second, "x", -1)
    partial = jnp.sum(exchange(partial, SECTION + LINE), axis=0)
    entering = exchange(after(arriving, partial), SECTION)

    first, second, yp_first, ym_second, xa, xb, partial, entering = together(
        (first, second, yp_first, ym_second, xa, xb, partial, entering)
    )
    pooled = jnp.sum(exchange(partial, PLANE), axis=0)
    yp_second = from_neighbour(second, "y", 1)
    ym_first = from_neighbour(first, "y", -1)
    xa_yp = from_neighbour(yp_first, "x", 1)
    xb_ym = from_neighbour(ym_second, "x", -1)
    pooled = pooled / prompt_tally[0].astype(f32)
    normed = pooled * lax.rsqrt(jnp.mean(pooled * pooled) + 1e-06)
    cond = jax.nn.silu(normed).astype(bf16).reshape(encoded)
    local = jnp.dot(adaptive_norm_weights, cond, preferred_element_type=f32)
    columns = local.shape[0]
    rows = -(-columns // LANES)
    local = jnp.pad(local, (0, rows * LANES - columns)).reshape(rows, LANES)
    line = exchange(local, LINE)
    mine = exchange(after(waiting, line), LINE)
    halves = [block[part] for block in (yp_first, ym_second) for part in (slice(middle), slice(middle, None))]

    line, mine, halves, yp_second, ym_first, xa_yp, xb_ym = together(
        (line, mine, halves, yp_second, ym_first, xa_yp, xb_ym)
    )
    y2 = [from_neighbour(halves[0], "y", 1), None, from_neighbour(halves[2], "y", -1), None]
    xa_ym = from_neighbour(ym_first, "x", 1)
    xb_yp = from_neighbour(yp_second, "x", -1)
    halves, y2[0], y2[2] = together((halves, y2[0], y2[2]))
    y2[1] = from_neighbour(halves[1], "y", 1)
    y2[3] = from_neighbour(halves[3], "y", -1)
    modes = exchange(line, PLANE)
    xa_yp_down = xa_yp[middle:]
    xb_ym_down = xb_ym[middle:]

    modes = modes.reshape(-1, rows * LANES)[:, :columns].reshape(3, -1)
    xa_y2_up = from_neighbour(y2[0], "x", 1)
    xb_y2_up = from_neighbour(y2[2], "x", -1)
    xa_y2_down = from_neighbour(xa_yp_down, "y", 1)
    xb_y2_down = from_neighbour(xb_ym_down, "y", -1)

    whole = [
        first, second, xa, xb, yp_first, ym_second, yp_second, ym_first, xa_yp, xb_ym, xa_ym, xb_yp
    ]
    count = len(whole)
    total = (count + 4) * middle
    main = (total - 1) // STEP * STEP
    cut = main - (count + 1) * middle
    plan = [
        (i, which * middle, middle, which, i * middle) for i in range(count) for which in (0, 1)
    ]
    plan += [(count + which, 0, middle, which, count * middle) for which in (0, 1)]
    plan += [(count + 2 + which, 0, cut, which, main - cut) for which in (0, 1)]
    up_rows, down_rows = place(plan, after(whole + y2, modes), main)
    theirs = lax.ppermute(after(mine, xa_ym, xb_yp), "xh", [(0, 1), (1, 0)])
    upper = lax.axis_index("xh") == 1
    gathered = jnp.stack([jnp.where(upper, theirs, mine), jnp.where(upper, mine, theirs)])
    plan = [(which, cut, middle - cut, which, 0) for which in (0, 1)]
    plan += [
        (2 + 2 * which + i, 0, middle, which, (1 + i) * middle - cut)
        for which in (0, 1)
        for i in (0, 1)
    ]
    ends = [y2[2], y2[3], xa_y2_up, xb_y2_up, xa_y2_down, xb_y2_down]
    up_end, down_end = place(plan, ends, total - main)
    return modes, gathered, entering, (up_rows, down_rows, up_end, down_end)


def per_device(
    travelling_inputs,
    travelling_region,
    arriving_tiles,
    arriving_region,
    prompt_embeddings,
    prompt_tally,
    adaptive_norm_weights,
    expansion_weights,
    contraction_weights,
):
    section_id = lax.axis_index(SECTION)
    is_first = section_id == 0
    tokens, breadth = travelling_inputs.shape[1:]

    def with_mask(values, region):
        column = jnp.broadcast_to(region.astype(bf16)[:, None], (tokens, LANES))
        return jnp.concatenate([values, column], axis=1)

    arriving = with_mask(arriving_tiles[0], arriving_region[0])
    waiting = with_mask(travelling_inputs[0], travelling_region[0])
    last = SECTIONS - 1
    mod, gathered, entering, weights = set_out(
        expansion_weights[0],
        contraction_weights[0],
        prompt_embeddings,
        prompt_tally,
        adaptive_norm_weights[0],
        travelling_inputs[0],
        arriving,
    )
    is_even = section_id % 2 == 0
    entering = [entering[section] for section in range(SECTIONS)]
    gathered, waiting, gate, entering, is_first, is_even = lax.optimization_barrier(
        (gathered, waiting, mod[2:], entering, is_first, is_even)
    )
    moves = []
    for tick in range(SECTIONS):
        if tick:
            gathered = exchange(waiting[:, :breadth], GROUP)
        partial = layer(gathered.reshape(GROUP_SIZE * tokens, breadth), mod, *weights)
        parts = lax.all_to_all(partial.reshape(GROUP_SIZE, tokens, breadth), GROUP, 0, 0)
        if tick == last:
            produced, held = after((produced, moves[0]), parts)
            third = jnp.where(is_first, held, produced)
            third = between_sections(third, [(last, 2, 1), (0, 0, 1)])
        produced = close(parts, waiting, gate)
        if tick < last:
            edges = [(0, 1, 0), (1, 2, 1), (2, 3, 0)]
            if tick < 2:
                edges.append((last, 0, 1))
        else:
            edges = [(0, 1, 0), (1, 2, 0), (2, 3, 1)]
        moves.append(between_sections(produced, edges))
        waiting = jnp.where(is_first, entering[tick], moves[tick])
    sent = jnp.where(is_first, moves[1], produced)
    second = between_sections(sent, [(0, 1, 1), (last, last, 1)])
    done = jnp.where(is_even, third, second)
    return done[None, :, :breadth], waiting[None, :, :breadth]


def solution(mesh):
    fine = Mesh(mesh.devices.reshape(tuple(SIZES.values())), tuple(SIZES))
    placed = (
        P(SECTION, TP, None),
        P(SECTION, TP),
        P(SECTION, TP, None),
        P(SECTION, TP),
        P(SECTION + TP, None),
        P(),
        P(SECTION, TP, None),
        P(SECTION, TP, None),
        P(SECTION, TP, None),
    )
    return jax.shard_map(
        per_device,
        mesh=fine,
        in_specs=placed,
        out_specs=(P(SECTION, TP, None), P(SECTION, TP, None)),
        check_vma=False,
    )
```

```python
import functools

import jax
import jax.numpy as jnp
import numpy as np
from jax import lax
from jax.experimental import pallas as pl
from jax.experimental.pallas import tpu as pltpu
from jax.sharding import Mesh, PartitionSpec as P

f32 = jnp.float32
bf16 = jnp.bfloat16

SIZES = {"zh": 2, "core": 2, "xh": 2, "xl": 2, "yh": 2, "yl": 2, "zc": 2, "zf": 2}
SECTION = ("zh", "core")
TP = ("xh", "xl", "yh", "yl", "zc", "zf")
PLANE = ("xh", "xl", "yh", "yl")
LINE = ("zc", "zf")
GROUP = ("xh",) + LINE
GROUP_SIZE = 8
SECTIONS = 4
LANES = 128
STEP = 256


def from_neighbour(block, axis, distance):
    route = [((i + distance) % 4, i) for i in range(4)]
    return lax.ppermute(block, (axis + "h", axis + "l"), route)


def between_sections(block, edges):
    route = [
        (2 * start + half, 2 * end + (half ^ flip)) for start, end, flip in edges for half in (0, 1)
    ]
    return lax.ppermute(block, SECTION + ("zc",), route)


def after(value, *earlier):
    return lax.optimization_barrier((value,) + earlier)[0]


def exchange(block, axes):
    count = int(np.prod([SIZES[a] for a in axes]))
    copies = jnp.broadcast_to(block[None], (count,) + block.shape)
    return lax.all_to_all(copies, axes, 0, 0)


def modulate(x_ref, mod_ref, inputs):
    values = x_ref[...].astype(f32)
    center = jnp.mean(values, axis=1, keepdims=True)
    moved = values - center
    spread = jnp.mean(moved * moved, axis=1, keepdims=True)
    inputs[...] = (
        moved * lax.rsqrt(spread + 1e-06) * (1.0 + mod_ref[1:2]) + mod_ref[0:1]
    ).astype(bf16)


def layer_kernel(x_ref, mod_ref, up, down, up_end, down_end, out_ref, inputs, hidden):
    modulate(x_ref, mod_ref, inputs)
    main = up.shape[0]
    total = main + up_end.shape[0]
    for at in range(0, total, STEP):
        rows = up[at : at + STEP] if at < main else up_end[at - main : at - main + STEP]
        raised = lax.dot_general(
            inputs[...], rows, (((1,), (1,)), ((), ())), preferred_element_type=f32
        )
        hidden[:, at : at + STEP] = jax.nn.gelu(raised, approximate=True).astype(bf16)
    for at in range(0, out_ref.shape[1], STEP):
        columns = slice(at, at + STEP)
        result = jnp.dot(hidden[:, :main], down[:, columns], preferred_element_type=f32)
        result += jnp.dot(hidden[:, main:], down_end[:, columns], preferred_element_type=f32)
        out_ref[:, columns] = result.astype(bf16)


def layer(tokens, mod, up, down, up_end, down_end):
    rows, breadth = tokens.shape
    total = up.shape[0] + up_end.shape[0]
    whole = pl.BlockSpec(memory_space=pltpu.VMEM)
    return pl.pallas_call(
        layer_kernel,
        out_shape=jax.ShapeDtypeStruct((rows, breadth), bf16),
        in_specs=[whole] * 6,
        out_specs=whole,
        scratch_shapes=[
            pltpu.VMEM((rows, breadth), bf16),
            pltpu.VMEM((rows, total), bf16),
        ],
        compiler_params=pltpu.CompilerParams(vmem_limit_bytes=24 * 1024 * 1024),
        cost_estimate=pl.CostEstimate(
            flops=4 * rows * total * breadth,
            bytes_accessed=4 * total * breadth + 4 * rows * breadth,
            transcendentals=rows * total,
        ),
    )(tokens, mod, up, down, up_end, down_end)


def place_kernel(plan, *refs):
    sem = refs[-1]
    outs = refs[-3:-1]
    copies = []
    for piece, first, rows, which, at in plan:
        copies.append(
            pltpu.make_async_copy(
                refs[piece].at[pl.ds(first, rows)],
                outs[which].at[pl.ds(at, rows)],
                sem.at[len(copies)],
            )
        )
    for copy in copies:
        copy.start()
    for copy in copies:
        copy.wait()


def place(plan, pieces, total):
    breadth = pieces[0].shape[1]
    whole = pl.BlockSpec(memory_space=pltpu.VMEM)
    return pl.pallas_call(
        functools.partial(place_kernel, plan),
        out_shape=[jax.ShapeDtypeStruct((total, breadth), bf16)] * 2,
        in_specs=[pl.BlockSpec(memory_space=pl.ANY)] * len(pieces),
        out_specs=[whole] * 2,
        scratch_shapes=[pltpu.SemaphoreType.DMA((len(plan),))],
        compiler_params=pltpu.CompilerParams(vmem_limit_bytes=20 * 1024 * 1024),
        cost_estimate=pl.CostEstimate(
            flops=0, bytes_accessed=8 * total * breadth, transcendentals=0
        ),
    )(*pieces)


def close_kernel(parts_ref, waiting_ref, gate_ref, out_ref):
    breadth = parts_ref.shape[2]
    result = parts_ref[0].astype(f32)
    for i in range(1, parts_ref.shape[0]):
        result += parts_ref[i].astype(f32)
    mask = waiting_ref[:, breadth:]
    kept = mask[:, :1].astype(f32)
    values = waiting_ref[:, :breadth].astype(f32)
    out_ref[:, :breadth] = (values + kept * gate_ref[...] * result).astype(bf16)
    out_ref[:, breadth:] = mask


def close(parts, waiting, gate):
    whole = pl.BlockSpec(memory_space=pltpu.VMEM)
    return pl.pallas_call(
        close_kernel,
        out_shape=jax.ShapeDtypeStruct(waiting.shape, waiting.dtype),
        in_specs=[whole] * 3,
        out_specs=whole,
        compiler_params=pltpu.CompilerParams(vmem_limit_bytes=4 * 1024 * 1024),
        cost_estimate=pl.CostEstimate(
            flops=parts.size, bytes_accessed=2 * parts.size, transcendentals=0
        ),
    )(parts, waiting, gate)


def set_out(up, down, prompt_embeddings, prompt_tally, adaptive_norm_weights, waiting, arriving):
    together = lax.optimization_barrier
    middle = up.shape[0] // 2
    first = jnp.concatenate([up[:middle], down[:middle]], axis=0)
    second = jnp.concatenate([up[middle:], down[middle:]], axis=0)
    count_rows, encoded = prompt_embeddings.shape
    first_row = lax.axis_index(SECTION + TP) * count_rows
    keep = (first_row + lax.iota(jnp.int32, count_rows) < prompt_tally[0]).astype(bf16)
    partial = jnp.dot(keep[None, :], prompt_embeddings, preferred_element_type=f32)
    partial = partial.reshape(encoded // LANES, LANES)

    first, second, partial = together((first, second, partial))
    yp_first = from_neighbour(first, "y", 1)
    ym_second = from_neighbour(second, "y", -1)
    xa = from_neighbour(first, "x", 1)
    xb = from_neighbour(second, "x", -1)
    partial = jnp.sum(exchange(partial, SECTION + LINE), axis=0)

    first, second, yp_first, ym_second, xa, xb, partial = together(
        (first, second, yp_first, ym_second, xa, xb, partial)
    )
    pooled = jnp.sum(exchange(partial, PLANE), axis=0)
    yp_second = from_neighbour(second, "y", 1)
    ym_first = from_neighbour(first, "y", -1)
    xa_yp = from_neighbour(yp_first, "x", 1)
    xb_ym = from_neighbour(ym_second, "x", -1)
    pooled = pooled / prompt_tally[0].astype(f32)
    normed = pooled * lax.rsqrt(jnp.mean(pooled * pooled) + 1e-06)
    cond = jax.nn.silu(normed).astype(bf16).reshape(encoded)
    local = jnp.dot(adaptive_norm_weights, cond, preferred_element_type=f32)
    columns = local.shape[0]
    rows = -(-columns // LANES)
    local = jnp.pad(local, (0, rows * LANES - columns)).reshape(rows, LANES)
    line = exchange(local, LINE)
    mine = exchange(after(waiting, line), LINE)
    halves = [block[part] for block in (yp_first, ym_second) for part in (slice(middle), slice(middle, None))]

    line, mine, halves, yp_second, ym_first, xa_yp, xb_ym = together(
        (line, mine, halves, yp_second, ym_first, xa_yp, xb_ym)
    )
    y2 = [from_neighbour(halves[0], "y", 1), None, from_neighbour(halves[2], "y", -1), None]
    xa_ym = from_neighbour(ym_first, "x", 1)
    xb_yp = from_neighbour(yp_second, "x", -1)
    halves, y2[0], y2[2] = together((halves, y2[0], y2[2]))
    y2[1] = from_neighbour(halves[1], "y", 1)
    y2[3] = from_neighbour(halves[3], "y", -1)
    entering = exchange(after(arriving, line), SECTION)
    modes = exchange(after(line, entering), PLANE)
    xa_yp_down = xa_yp[middle:]
    xb_ym_down = xb_ym[middle:]

    modes = modes.reshape(-1, rows * LANES)[:, :columns].reshape(3, -1)
    xa_y2_up = from_neighbour(y2[0], "x", 1)
    xb_y2_up = from_neighbour(y2[2], "x", -1)
    xa_y2_down = from_neighbour(xa_yp_down, "y", 1)
    xb_y2_down = from_neighbour(xb_ym_down, "y", -1)

    whole = [
        first, second, xa, xb, yp_first, ym_second, yp_second, ym_first, xa_yp, xb_ym, xa_ym, xb_yp
    ]
    count = len(whole)
    total = (count + 4) * middle
    main = (total - 1) // STEP * STEP
    cut = main - (count + 1) * middle
    plan = [
        (i, which * middle, middle, which, i * middle) for i in range(count) for which in (0, 1)
    ]
    plan += [(count + which, 0, middle, which, count * middle) for which in (0, 1)]
    plan += [(count + 2 + which, 0, cut, which, main - cut) for which in (0, 1)]
    up_rows, down_rows = place(plan, after(whole + y2, modes), main)
    theirs = lax.ppermute(after(mine, xa_ym, xb_yp), "xh", [(0, 1), (1, 0)])
    upper = lax.axis_index("xh") == 1
    gathered = jnp.stack([jnp.where(upper, theirs, mine), jnp.where(upper, mine, theirs)])
    plan = [(which, cut, middle - cut, which, 0) for which in (0, 1)]
    plan += [
        (2 + 2 * which + i, 0, middle, which, (1 + i) * middle - cut)
        for which in (0, 1)
        for i in (0, 1)
    ]
    ends = [y2[2], y2[3], xa_y2_up, xb_y2_up, xa_y2_down, xb_y2_down]
    up_end, down_end = place(plan, ends, total - main)
    return modes, gathered, entering, (up_rows, down_rows, up_end, down_end)


def per_device(
    travelling_inputs,
    travelling_region,
    arriving_tiles,
    arriving_region,
    prompt_embeddings,
    prompt_tally,
    adaptive_norm_weights,
    expansion_weights,
    contraction_weights,
):
    section_id = lax.axis_index(SECTION)
    is_first = section_id == 0
    tokens, breadth = travelling_inputs.shape[1:]

    def with_mask(values, region):
        column = jnp.broadcast_to(region.astype(bf16)[:, None], (tokens, LANES))
        return jnp.concatenate([values, column], axis=1)

    arriving = with_mask(arriving_tiles[0], arriving_region[0])
    waiting = with_mask(travelling_inputs[0], travelling_region[0])
    last = SECTIONS - 1
    mod, gathered, entering, weights = set_out(
        expansion_weights[0],
        contraction_weights[0],
        prompt_embeddings,
        prompt_tally,
        adaptive_norm_weights[0],
        travelling_inputs[0],
        arriving,
    )
    is_third = section_id == 2
    entering = [entering[section] for section in range(SECTIONS)]
    gathered, waiting, gate, entering, is_first, is_third = lax.optimization_barrier(
        (gathered, waiting, mod[2:], entering, is_first, is_third)
    )
    moves = []
    for tick in range(SECTIONS):
        if tick:
            gathered = exchange(waiting[:, :breadth], GROUP)
        partial = layer(gathered.reshape(GROUP_SIZE * tokens, breadth), mod, *weights)
        parts = lax.all_to_all(partial.reshape(GROUP_SIZE, tokens, breadth), GROUP, 0, 0)
        if tick == last:
            third = between_sections(after(produced, parts), [(last, 2, 1)])
        produced = close(parts, waiting, gate)
        if tick < last:
            edges = [(0, 1, 0), (1, 2, 1), (2, 3, 0)]
            if tick < 2:
                edges.append((last, 0, 0))
        else:
            edges = [(0, 1, 0), (1, 2, 0), (2, 3, 1)]
        moves.append(between_sections(produced, edges))
        waiting = jnp.where(is_first, entering[tick], moves[tick])
    sent = jnp.where(is_first, moves[1], produced)
    second = between_sections(sent, [(0, 1, 0), (last, last, 1)])
    done = jnp.where(is_first, moves[0], jnp.where(is_third, third, second))
    return done[None, :, :breadth], waiting[None, :, :breadth]


def solution(mesh):
    fine = Mesh(mesh.devices.reshape(tuple(SIZES.values())), tuple(SIZES))
    placed = (
        P(SECTION, TP, None),
        P(SECTION, TP),
        P(SECTION, TP, None),
        P(SECTION, TP),
        P(SECTION + TP, None),
        P(),
        P(SECTION, TP, None),
        P(SECTION, TP, None),
        P(SECTION, TP, None),
    )
    return jax.shard_map(
        per_device,
        mesh=fine,
        in_specs=placed,
        out_specs=(P(SECTION, TP, None), P(SECTION, TP, None)),
        check_vma=False,
    )
```
